128 devices in a mesh: row: 16 (over z, x), col: 8 (over y, core).
Axes of the slice: x: 4, y: 4, z: 4, core: 2. Of those that a mesh axis runs over, the one named last changes fastest.
Arguments:
- matrix_blocks: float32 [8, 16, 16, 8, 128, 128], P(None, 'row', None, 'col'), as said below
- pattern: int32 [128, 128], replicated, may hold values from 0 to 1, as said below
- order: int32 [128], replicated, may hold values from 0 to 127, each once
Outputs:
- panels: bfloat16 [2, 8, 16, 128, 512], P(None, None, 'row')
- trailing: float32 [8, 16, 16, 8, 128, 128], P(None, 'row', None, 'col')
The draws below stay inside these ranges and needn't reach their ends.
Inputs may be any that keep to these rules, and one draw needn't show every extreme that they name: The blocks fall into 8 nonempty clusters, and pattern[g, h] is 1 exactly where blocks g and h lie in the same cluster. `matrix_blocks`: symmetric as a 16384 x 16384 matrix and positive definite, also after masking by any such pattern.
All inputs are finite; a program needn't handle non-finite values.
Results may differ from the reference program's by a relative error of at most 0.0022.
Values may be sent and summed in bfloat16 or wider, within the bound.
A program may use at most 128 MiB of HBM per device.

```python
import jax
import jax.numpy as jnp
from jax import lax

BLOCK = 128
SUPER = 4
RB_DEV = 8
NB = 128
CB_DEV = 16
NDOF = 16384
N_ROW = 16
N_COL = 8


def draw_matrix_blocks(key, part):
    key = jax.random.fold_in(key, 11)
    first = jax.random.fold_in(key, 0)
    feature_count = 8 * BLOCK
    raw_features = jnp.clip(jax.random.normal(first, (NDOF, feature_count), jnp.float32), -5.0, 5.0)
    coupled = jnp.dot(raw_features, raw_features.T, precision=lax.Precision.HIGHEST) / feature_count
    coupled = (coupled + coupled.T) * 0.5
    position = jnp.arange(NDOF)
    coupled = coupled + jnp.where(position[:, None] == position[None, :], 0.25, 0.0)
    whole_matrix = coupled
    return whole_matrix.reshape(RB_DEV, N_ROW, BLOCK, CB_DEV, N_COL, BLOCK).transpose(0, 1, 3, 4, 2, 5)


def draw_pattern(key, part):
    key = jax.random.fold_in(key, 23)
    first, second = jax.random.split(key)
    cluster_count = max(NB // 16, 2)
    ranking = jax.random.permutation(first, NB).astype(jnp.int32)
    picks = jax.random.randint(second, (NB,), 0, cluster_count).astype(jnp.int32)
    labels = jnp.where(ranking < cluster_count, ranking, picks)
    return (labels[:, None] == labels[None, :]).astype(jnp.int32)


def setup_inputs(seed: int = 0) -> dict:
    keys = jax.random.split(jax.random.key(seed), 4)
    return {
        "matrix_blocks": draw_matrix_blocks(jax.random.fold_in(keys[3], 71), 0),
        "pattern": draw_pattern(jax.random.fold_in(keys[3], 71), 0),
        "order": jax.random.permutation(keys[2], NB).astype(jnp.int32),
    }


def reference(matrix_blocks, pattern, order):
    full = matrix_blocks.transpose(0, 1, 4, 2, 3, 5).reshape(NB, BLOCK, NB, BLOCK)
    full = full * pattern.astype(jnp.float32)[:, None, :, None]
    full = full.reshape(NDOF, NDOF)
    dead = jnp.zeros((NB,), jnp.float32)
    outputs = []
    for step in range(2):
        chosen = order[step * SUPER:(step + 1) * SUPER].astype(jnp.int32)
        columns = (chosen[:, None] * BLOCK + jnp.arange(BLOCK, dtype=jnp.int32)[None, :]).reshape(-1)
        panel = jnp.take(full, columns, axis=1)
        square = jnp.take(panel, columns, axis=0)
        factor = jnp.linalg.cholesky(square)
        lower = lax.linalg.triangular_solve(factor, panel, left_side=False, lower=True, transpose_a=True)
        dead = dead.at[chosen].set(1.0)
        alive = jnp.repeat(1.0 - dead, BLOCK)
        rounded = (lower * alive[:, None]).astype(jnp.bfloat16)
        outputs.append(rounded.reshape(RB_DEV, N_ROW, BLOCK, SUPER * BLOCK))
        full = full - jnp.dot(rounded.astype(jnp.float32), rounded.T.astype(jnp.float32), preferred_element_type=jnp.float32)
    trailing = full.reshape(RB_DEV, N_ROW, BLOCK, CB_DEV, N_COL, BLOCK).transpose(0, 1, 3, 4, 2, 5)
    return (jnp.stack(outputs), trailing)
```

```python
import functools

import jax
import jax.numpy as jnp
from jax import lax
from jax.experimental import pallas as pl
from jax.experimental.pallas import tpu as pltpu
from jax.sharding import PartitionSpec as P

SUPER = 4
PICKS = 8
KR = 24
KD = 24
MESH = pl.DeviceIdType.MESH
HIGH = lax.Precision.HIGHEST
F32 = jnp.float32
BF16 = jnp.bfloat16
NT = (((1,), (1,)), ((), ()))

POS = 0
POSC = 64
ALIVE = 192
SAME = 256
POSD = 320
TARGET = 384
LEVEL = 392
FIRST = 400
DEPTH = 408
HIT = 416


def dot_nt(a, b):
    return lax.dot_general(a, b, NT, precision=HIGH, preferred_element_type=F32)


def pick_kernel(meta, a_ref, out_ref, sems):
    my_col = lax.axis_index("col")
    out_ref[...] = jnp.zeros_like(out_ref)

    def copy(p):
        slot = jnp.maximum(meta[POS + p], 0)
        target = meta[TARGET + p % PICKS]
        mine = (meta[POS + p] >= 0) & (target % 8 == my_col)
        return mine, pltpu.make_async_copy(
            a_ref.at[p // PICKS, target // 8], out_ref.at[:, slot], sems.at[slot]
        )

    @pl.loop(0, 64)
    def _(p):
        mine, c = copy(p)

        @pl.when(mine)
        def _():
            c.start()

    @pl.loop(0, 64)
    def _(p):
        mine, c = copy(p)

        @pl.when(mine)
        def _():
            c.wait()


def pick(meta, blocks):
    return pl.pallas_call(
        pick_kernel,
        out_shape=jax.ShapeDtypeStruct((8, KR, 16, 128), F32),
        in_specs=[pl.BlockSpec(memory_space=pltpu.SMEM), pl.BlockSpec(memory_space=pl.ANY)],
        out_specs=pl.BlockSpec(memory_space=pltpu.VMEM),
        scratch_shapes=[pltpu.SemaphoreType.DMA((KR,))],
        compiler_params=pltpu.CompilerParams(vmem_limit_bytes=16 << 20),
        name="pick",
    )(meta, blocks)


def place():
    r = lax.axis_index("row")
    c = lax.axis_index("col")
    return r, c, c // 2, c % 2


def gather_kernel(
    dl_ref, give_ref, x_ref, d_ref, ra, acc, rb, dsrc, rr, piece,
    sa, qa, sb, qb, sc, qc, sd, qd, se, qe, sf, qf,
):
    r, c, y, k = place()
    other = {"row": r, "col": y * 2 + 1 - k}

    def along(dy):
        return {"row": r, "col": lax.rem(y + dy, 4) * 2 + k}

    def across(dr):
        return {"row": lax.rem(r + dr, 16), "col": c}

    barrier = pltpu.get_barrier_semaphore()
    pl.semaphore_signal(barrier, inc=1, device_id=other, device_id_type=MESH)
    for dy in (1, 2, 3):
        pl.semaphore_signal(barrier, inc=1, device_id=along(dy), device_id_type=MESH)
    for dr in range(1, 16):
        pl.semaphore_signal(barrier, inc=1, device_id=across(dr), device_id_type=MESH)
    pl.semaphore_wait(barrier, 19)

    halves = []
    for dy in (2, 1, 3, 0):
        there = lax.rem(y + dy, 4)
        h = pltpu.make_async_remote_copy(
            src_ref=give_ref.at[there, 1 - k], dst_ref=ra.at[dy],
            send_sem=sa.at[dy], recv_sem=qa.at[dy], device_id=other, device_id_type=MESH,
        )
        h.start()
        halves.append((dy, there, h))
    quarters = []
    for dy, there, h in halves:
        h.wait_recv()
        if dy:
            acc[dy] = give_ref[there, k] + ra[dy]
            q = pltpu.make_async_remote_copy(
                src_ref=acc.at[dy], dst_ref=rb.at[dy],
                send_sem=sb.at[dy], recv_sem=qb.at[dy], device_id=along(dy), device_id_type=MESH,
            )
            q.start()
            quarters.append((dy, q))
        else:
            total = give_ref[there, k] + ra[dy]
    for dy, q in quarters:
        q.wait_recv()
        total = total + rb[dy]
    x_ref[...] = total

    for d in range(KD):
        code = dl_ref[d]
        mine = (code // 64 == r).astype(F32)
        dsrc[d * 16 : (d + 1) * 16] = x_ref[code % 64] * mine
    parts = []
    for dr in range(1, 16):
        there = lax.rem(r + dr, 16)
        h = pltpu.make_async_remote_copy(
            src_ref=dsrc.at[pl.ds(there * KD, KD)], dst_ref=rr.at[dr],
            send_sem=sc.at[dr], recv_sem=qc.at[dr], device_id=across(dr), device_id_type=MESH,
        )
        h.start()
        parts.append(h)
    total = dsrc[pl.ds(pl.multiple_of(r * KD, 8), KD)]
    for dr, h in zip(range(1, 16), parts):
        h.wait_recv()
        total = total + rr[dr]
    piece[...] = total
    mine = pl.ds(pl.multiple_of(r * KD, 8), KD)
    d_ref[y, k, mine] = total
    wholes = []
    for dr in range(1, 16):
        h = pltpu.make_async_remote_copy(
            src_ref=piece, dst_ref=d_ref.at[y, k, mine],
            send_sem=sd.at[dr], recv_sem=qd.at[dr], device_id=across(dr), device_id_type=MESH,
        )
        h.start()
        wholes.append(h)
    for h in wholes:
        h.wait_recv()
    spread(d_ref, along, other, y, k, se, qe, sf, qf)
    for _, _, h in halves:
        h.wait_send()
    for _, q in quarters:
        q.wait_send()
    for h in parts + wholes:
        h.wait_send()


def spread(ref, along, other, y, k, se, qe, sf, qf):
    outs = []
    for dy in (2, 1, 3):
        h = pltpu.make_async_remote_copy(
            src_ref=ref.at[y, k], dst_ref=ref.at[y, k],
            send_sem=se.at[dy], recv_sem=qe.at[dy], device_id=along(dy), device_id_type=MESH,
        )
        h.start()
        outs.append((dy, h))
    twins = []
    for dy in (0, 1, 3, 2):
        come = lax.rem(y + 4 - dy, 4)
        for d, h in outs:
            if d == dy:
                h.wait_recv()
        t = pltpu.make_async_remote_copy(
            src_ref=ref.at[come, k], dst_ref=ref.at[come, k],
            send_sem=sf.at[dy], recv_sem=qf.at[dy], device_id=other, device_id_type=MESH,
        )
        t.start()
        twins.append(t)
    for t in twins:
        t.wait()
    for _, h in outs:
        h.wait_send()


def gather(dl, given):
    vmem = pl.BlockSpec(memory_space=pltpu.VMEM)
    dma = pltpu.SemaphoreType.DMA
    return pl.pallas_call(
        gather_kernel,
        out_shape=(
            jax.ShapeDtypeStruct((KR, 16, 128), F32),
            jax.ShapeDtypeStruct((4, 2, KD * 16, 128), F32),
        ),
        in_specs=[pl.BlockSpec(memory_space=pltpu.SMEM), vmem],
        out_specs=(vmem, vmem),
        scratch_shapes=[
            pltpu.VMEM((4, KR, 16, 128), F32),
            pltpu.VMEM((4, KR, 16, 128), F32),
            pltpu.VMEM((4, KR, 16, 128), F32),
            pltpu.VMEM((KD * 16, 128), F32),
            pltpu.VMEM((16, KD, 128), F32),
            pltpu.VMEM((KD, 128), F32),
            dma((4,)), dma((4,)), dma((4,)), dma((4,)),
            dma((16,)), dma((16,)), dma((16,)), dma((16,)),
            dma((4,)), dma((4,)), dma((4,)), dma((4,)),
        ],
        compiler_params=pltpu.CompilerParams(
            collective_id=0, has_side_effects=True, vmem_limit_bytes=32 << 20
        ),
        name="gather",
    )(dl, given.reshape(4, 2, KR, 16, 128))


def lane(x, i):
    return jnp.take_along_axis(x, jnp.full(x.shape, i, jnp.int32), axis=1)


def batched_inverse(sb, gb):
    @pl.loop(0, 16)
    def _(c):
        base = pl.multiple_of(c * 64, 64)
        e = {}
        for i in range(8):
            row = sb[pl.ds(base + i * 8, 8)]
            for k in range(i + 1):
                e[i, k] = lane(row, c * 8 + k)
        f = {}
        for k in range(8):
            f[k, k] = lax.rsqrt(e[k, k])
            for i in range(k + 1, 8):
                f[i, k] = e[i, k] * f[k, k]
            for i in range(k + 1, 8):
                for m in range(k + 1, i + 1):
                    e[i, m] = e[i, m] - f[i, k] * f[m, k]
        us, vs = [], []
        for k in range(8):
            u = sb[pl.ds(base + k * 8, 8)]
            v = gb[pl.ds(base + k * 8, 8)]
            for m in range(k):
                u = u - f[k, m] * us[m]
                v = v - f[k, m] * vs[m]
            us.append(u * f[k, k])
            vs.append(v * f[k, k])
        for k in range(8):
            gb[pl.ds(base + k * 8, 8)] = vs[k]

        @pl.loop(c + 1, 16)
        def _(q):
            low = pl.multiple_of(q * 64, 64)
            for m in range(8):
                here = pl.ds(low + m * 8, 8)
                u = sb[here]
                v = gb[here]
                for k in range(8):
                    w = lane(us[k], q * 8 + m)
                    u = u - w * us[k]
                    v = v - w * vs[k]
                sb[here] = u
                gb[here] = v


def factor_kernel(meta, x_ref, d_ref, out_ref, sb, gb, g, f, s, w, ld):
    def same(i, j):
        return meta[SAME + i * PICKS + j] > 0

    def held(value, i, j):
        return jnp.where(i // SUPER < j // SUPER, value.astype(BF16).astype(F32), value)

    def block(i, j):
        return d_ref[:, meta[POSD + i * PICKS + j]].reshape(128, 128)

    lanes = lax.broadcasted_iota(jnp.int32, (8, 128), 1)

    @pl.loop(0, meta[DEPTH])
    def _(level):
        @pl.loop(0, 128)
        def _(i):
            unit = (lanes == i).astype(F32)
            here = pl.ds(pl.multiple_of(i * 8, 8), 8)
            sb[here] = unit
            gb[here] = unit

        @pl.loop(0, PICKS)
        def _(j):
            @pl.when(meta[LEVEL + j] == level)
            def _():
                s[...] = block(j, j)

                @pl.loop(0, j)
                def _(i):
                    @pl.when(same(j, i))
                    def _():
                        w[...] = block(j, i)

                        @pl.loop(0, i)
                        def _(m):
                            @pl.when(same(j, m))
                            def _():
                                w[...] -= dot_nt(
                                    held(f[j * PICKS + m], m, i), held(f[i * PICKS + m], m, i)
                                )

                        done = dot_nt(w[...], g[i])
                        f[j * PICKS + i] = done
                        done = held(done, i, j)
                        s[...] -= dot_nt(done, done)

                sb[pl.ds(meta[FIRST + j], 128, stride=8)] = s[...]

        batched_inverse(sb, gb)

        @pl.loop(0, PICKS)
        def _(j):
            @pl.when(meta[LEVEL + j] == level)
            def _():
                g[j] = gb[pl.ds(meta[FIRST + j], 128, stride=8)]

    ld[...] = jnp.zeros_like(ld)
    out_ref[...] = jnp.zeros_like(out_ref)

    @pl.loop(0, 64)
    def _(p):
        @pl.when(meta[POS + p] >= 0)
        def _():
            a = pl.multiple_of(p // PICKS * 16, 16)
            ld[p % PICKS, pl.ds(a, 16)] = x_ref[meta[POS + p]]

    @pl.loop(0, PICKS)
    def _(j):
        @pl.loop(0, j)
        def _(i):
            @pl.when(same(j, i))
            def _():
                ld[j] -= dot_nt(held(ld[i], i, j), held(f[j * PICKS + i], i, j))

        ld[j] = dot_nt(ld[j], g[j])

    @pl.loop(0, 64)
    def _(p):
        @pl.when((meta[POS + p] >= 0) & (meta[ALIVE + p] > 0))
        def _():
            a = pl.multiple_of(p // PICKS * 16, 16)
            out_ref[meta[POS + p]] = ld[p % PICKS, pl.ds(a, 16)].astype(BF16)


def factor(meta, x, d):
    vmem = pl.BlockSpec(memory_space=pltpu.VMEM)
    return pl.pallas_call(
        factor_kernel,
        out_shape=jax.ShapeDtypeStruct((KR, 16, 128), BF16),
        in_specs=[pl.BlockSpec(memory_space=pltpu.SMEM), vmem, vmem],
        out_specs=vmem,
        scratch_shapes=[
            pltpu.VMEM((1024, 128), F32),
            pltpu.VMEM((1024, 128), F32),
            pltpu.VMEM((8, 128, 128), F32),
            pltpu.VMEM((64, 128, 128), F32),
            pltpu.VMEM((128, 128), F32),
            pltpu.VMEM((128, 128), F32),
            pltpu.VMEM((8, 128, 128), F32),
        ],
        compiler_params=pltpu.CompilerParams(vmem_limit_bytes=32 << 20),
        name="factor",
    )(meta, x, d.reshape(8, KD, 16, 128))


def share_kernel(l_ref, row_ref, col_ref, se, qe, sf, qf, sg, qg, here):
    r, c, y, k = place()
    other = {"row": r, "col": y * 2 + 1 - k}
    goal = lax.rem(r, 8)
    high = r // 8

    def along(dy):
        return {"row": r, "col": lax.rem(y + dy, 4) * 2 + k}

    barrier = pltpu.get_barrier_semaphore()
    pl.semaphore_signal(barrier, inc=1, device_id=other, device_id_type=MESH)
    for dy in (1, 2, 3):
        pl.semaphore_signal(barrier, inc=1, device_id=along(dy), device_id_type=MESH)
    for q in range(16):
        source = c + (q // 8) * 8
        far = jnp.logical_not((source == r) & (q % 8 == c))

        @pl.when(far)
        def _():
            pl.semaphore_signal(
                barrier, inc=1, device_id={"row": source, "col": q % 8}, device_id_type=MESH
            )

    pl.semaphore_wait(barrier, 19 + jnp.where(goal == c, 0, 1))

    def send(dr):
        return pltpu.make_async_remote_copy(
            src_ref=l_ref, dst_ref=col_ref.at[high, y, k],
            send_sem=sg.at[dr], recv_sem=qg.at[high * 8 + c],
            device_id={"row": lax.rem(r + dr, 16), "col": goal}, device_id_type=MESH,
        )

    for dr in range(1, 16):
        send(dr).start()
    keep = pltpu.make_async_copy(l_ref, col_ref.at[high, y, k], here.at[0])

    @pl.when(goal == c)
    def _():
        keep.start()

    @pl.when(goal != c)
    def _():
        send(0).start()

    row_ref[y, k] = l_ref[...]
    spread(row_ref, along, other, y, k, se, qe, sf, qf)

    for q in range(16):
        source = c + (q // 8) * 8
        far = jnp.logical_not((source == r) & (q % 8 == c))

        @pl.when(far)
        def _():
            pltpu.make_async_remote_copy(
                src_ref=l_ref, dst_ref=col_ref.at[q // 8, (q % 8) // 2, q % 2],
                send_sem=sg.at[0], recv_sem=qg.at[q],
                device_id=other, device_id_type=MESH,
            ).wait_recv()

    for dr in range(1, 16):
        send(dr).wait_send()

    @pl.when(goal == c)
    def _():
        keep.wait()

    @pl.when(goal != c)
    def _():
        send(0).wait_send()


def share(l):
    vmem = pl.BlockSpec(memory_space=pltpu.VMEM)
    dma = pltpu.SemaphoreType.DMA
    return pl.pallas_call(
        share_kernel,
        out_shape=(
            jax.ShapeDtypeStruct((4, 2, KR, 16, 128), BF16),
            jax.ShapeDtypeStruct((2, 4, 2, KR, 16, 128), BF16),
        ),
        in_specs=[vmem],
        out_specs=(vmem, vmem),
        scratch_shapes=[
            dma((4,)), dma((4,)), dma((4,)), dma((4,)), dma((16,)), dma((16,)), dma((1,)),
        ],
        compiler_params=pltpu.CompilerParams(
            collective_id=1, has_side_effects=True, vmem_limit_bytes=32 << 20
        ),
        name="share",
    )(l)


def update_kernel(meta, a_ref, row_ref, col_ref, panel_ref, out_ref):
    a = pl.program_id(0)
    for j in range(PICKS):
        slot = meta[POS + a * PICKS + j]
        lanes = slice((j % SUPER) * 128, (j % SUPER + 1) * 128)

        @pl.when(slot >= 0)
        def _():
            panel_ref[j // SUPER, 0, :, lanes] = row_ref[:, slot].reshape(128, 128)

        @pl.when(slot < 0)
        def _():
            panel_ref[j // SUPER, 0, :, lanes] = jnp.zeros((128, 128), BF16)

    for b in range(16):
        hit = meta[HIT + a * 16 + b] > 0

        @pl.when(hit)
        def _():
            out_ref[0, b] = a_ref[0, b]

            @pl.loop(0, PICKS)
            def _(j):
                slot = meta[POS + a * PICKS + j]

                @pl.when(slot >= 0)
                def _():
                    left = row_ref[:, slot].reshape(128, 128)
                    down = meta[POSC + (b % 2) * 64 + (b // 2) * PICKS + j]
                    right = col_ref[b % 2, :, jnp.maximum(down, 0)].reshape(128, 128)
                    out_ref[0, b] -= lax.dot_general(left, right, NT, preferred_element_type=F32)

        @pl.when(jnp.logical_not(hit))
        def _():
            out_ref[0, b] = jnp.zeros((128, 128), F32)


def update(meta, blocks, rows, cols):
    whole = lambda n: (lambda a, m: (0,) * n)
    return pl.pallas_call(
        update_kernel,
        grid_spec=pltpu.PrefetchScalarGridSpec(
            num_scalar_prefetch=1,
            grid=(8,),
            in_specs=[
                pl.BlockSpec((1, 16, 128, 128), lambda a, m: (a, 0, 0, 0)),
                pl.BlockSpec((8, KR, 16, 128), whole(4)),
                pl.BlockSpec((2, 8, KR, 16, 128), whole(5)),
            ],
            out_specs=[
                pl.BlockSpec((2, 1, 128, 512), lambda a, m: (0, a, 0, 0)),
                pl.BlockSpec((1, 16, 128, 128), lambda a, m: (a, 0, 0, 0)),
            ],
        ),
        out_shape=(
            jax.ShapeDtypeStruct((2, 8, 128, 512), BF16),
            jax.ShapeDtypeStruct((8, 16, 128, 128), F32),
        ),
        compiler_params=pltpu.CompilerParams(vmem_limit_bytes=32 << 20),
        name="update",
    )(meta, blocks, rows.reshape(8, KR, 16, 128), cols.reshape(2, 8, KR, 16, 128))


def tables(pattern, order, my_row, my_col):
    target = order[:PICKS]
    blocks = jnp.arange(128, dtype=jnp.int32)
    onehot = (target[:, None] == blocks[None, :]).astype(F32)
    linked = pattern.astype(F32)
    member = jnp.dot(onehot, linked)
    among = jnp.dot(member, onehot.T)
    index = jnp.arange(64, dtype=jnp.int32)
    before = (index[:, None] < index[None, :]).astype(F32)
    own = member.reshape(PICKS, 8, 16).transpose(2, 1, 0).reshape(16, 64)
    rank = jnp.dot(own, before)
    slot = jnp.where(own > 0, rank, -1.0)
    full = jnp.max(jnp.sum(own, axis=1))
    small = jnp.arange(PICKS)
    low = (small[None, :] <= small[:, None])
    ed = (among.T * low).reshape(1, 64)
    rankd = jnp.dot(ed, before)
    fulld = jnp.sum(ed)
    ed2 = ed.reshape(PICKS, PICKS)
    level = jnp.sum(ed2, axis=1).astype(jnp.int32) - 1
    first = jnp.min(jnp.where(ed2 > 0, small[None, :], PICKS), axis=1).astype(jnp.int32)
    by_block = slot.reshape(16, 8, PICKS).transpose(1, 0, 2).reshape(128, PICKS)
    where_d = jnp.dot(onehot, by_block)
    code = (target % 16)[:, None] * 64 + where_d.astype(jnp.int32)
    code = jnp.where(ed2 > 0, code, 0).reshape(64)
    rankd = jnp.where(ed > 0, rankd, -1.0).astype(jnp.int32).reshape(64)
    slots = jnp.arange(KD, dtype=jnp.int32)
    match = rankd[None, :] == slots[:, None]
    dl = jnp.where(
        slots < fulld.astype(jnp.int32),
        jnp.sum(jnp.where(match, code[None, :], 0), axis=1),
        16 * 64,
    )
    dead = jnp.stack([jnp.sum(onehot[:SUPER], axis=0), jnp.sum(onehot, axis=0)])
    alive = 1.0 - lax.dynamic_index_in_dim(dead.reshape(2, 8, 16), my_row, 2, keepdims=False)
    alive = jnp.repeat(alive.T, SUPER, axis=1).reshape(64).astype(jnp.int32)
    slot = slot.astype(jnp.int32)
    hit = lax.dynamic_index_in_dim(pattern.reshape(8, 16, 128), my_row, 1, keepdims=False)
    hit = lax.dynamic_index_in_dim(hit.reshape(8, 16, 8), my_col, 2, keepdims=False)
    pick_row = lambda i: lax.dynamic_index_in_dim(slot, i, 0, keepdims=False)
    meta = jnp.concatenate(
        [
            pick_row(my_row), pick_row(my_col), pick_row(my_col + 8), alive,
            ed.astype(jnp.int32).reshape(64), jnp.maximum(rankd, 0),
            target, level, first, jnp.full((8,), jnp.max(level) + 1), hit.reshape(128),
        ]
    ).astype(jnp.int32)
    fits = (full <= KR) & (fulld <= KD)
    return meta, dl.astype(jnp.int32), fits


def compact(meta, dl, blocks):
    given = pick(meta, blocks.reshape(8, 16, 8, 16, 128))
    x, d = gather(dl, given)
    l = factor(meta, x, d)
    rows, cols = share(l)
    return update(meta, blocks, rows, cols)


def broadcast(value, axis, source):
    kept = jnp.where(lax.axis_index(axis) == source, value, 0).astype(value.dtype)
    return lax.psum(kept, axis)


def dense(pattern, order, local):
    rows_axis = lax.axis_size("row")
    cols_axis = lax.axis_size("col")
    my_row = lax.axis_index("row")
    my_col = lax.axis_index("col")
    row_blocks, col_blocks, _, width = local.shape
    ratio = rows_axis // cols_axis
    total_blocks = row_blocks * rows_axis
    my_pattern = lax.dynamic_index_in_dim(
        pattern.reshape(row_blocks, rows_axis, total_blocks), my_row, 1, keepdims=False
    )
    my_pattern = lax.dynamic_index_in_dim(
        my_pattern.reshape(row_blocks, col_blocks, cols_axis), my_col, 2, keepdims=False
    )
    current = local * my_pattern.astype(F32)[:, :, None, None]
    dead = jnp.zeros((total_blocks,), F32)
    results = []
    for step in range(2):
        chosen = order[step * SUPER : (step + 1) * SUPER]
        pieces = []
        for member in range(SUPER):
            target = chosen[member]
            column_here = lax.dynamic_index_in_dim(current, target // cols_axis, 1, keepdims=False)
            pieces.append(broadcast(column_here, "col", target % cols_axis))
        panel = jnp.concatenate(pieces, axis=2)
        parts_list = []
        for member in range(SUPER):
            target = chosen[member]
            row_here = lax.dynamic_index_in_dim(panel, target // rows_axis, 0, keepdims=False)
            parts_list.append(
                jnp.where(target % rows_axis == my_row, row_here, jnp.zeros_like(row_here))
            )
        square = lax.psum(jnp.concatenate(parts_list, axis=0), "row")
        factored = jnp.linalg.cholesky(square)
        flat = panel.reshape(row_blocks * width, SUPER * width)
        lower = lax.linalg.triangular_solve(
            factored, flat, left_side=False, lower=True, transpose_a=True
        )
        dead = dead.at[chosen].set(1.0)
        alive = lax.dynamic_index_in_dim(
            (1.0 - dead).reshape(row_blocks, rows_axis), my_row, 1, keepdims=False
        )
        rounded = (lower.reshape(row_blocks, width, SUPER * width) * alive[:, None, None]).astype(
            BF16
        )
        results.append(rounded)
        whole = lax.all_gather(rounded, "row", axis=0, tiled=True)
        whole = whole.reshape(ratio, cols_axis, row_blocks, width, SUPER * width)
        picked = lax.dynamic_index_in_dim(whole, my_col, 1, keepdims=False)
        column_panel = picked.transpose(1, 0, 2, 3).reshape(col_blocks, width, SUPER * width)
        change = jnp.einsum("aik,cjk->acij", rounded, column_panel, preferred_element_type=F32)
        current = current - change
    return jnp.stack(results), current


def shards(matrix_blocks, pattern, order):
    local = matrix_blocks[:, 0, :, 0]
    meta, dl, fits = tables(pattern, order, lax.axis_index("row"), lax.axis_index("col"))
    panels, trailing = lax.cond(
        fits,
        lambda: compact(meta, dl, local),
        lambda: dense(pattern, order, local),
    )
    return panels[:, :, None], trailing[:, None, :, None]


def solution(mesh):
    in_specs = (P(None, "row", None, "col", None, None), P(), P())
    out_specs = (P(None, None, "row", None, None), P(None, "row", None, "col", None, None))
    return jax.shard_map(shards, mesh=mesh, in_specs=in_specs, out_specs=out_specs, check_vma=False)
```

```python
import functools

import jax
import jax.numpy as jnp
from jax import lax
from jax.experimental import pallas as pl
from jax.experimental.layout import Layout, with_layout_constraint
from jax.experimental.pallas import tpu as pltpu
from jax.sharding import PartitionSpec as P

SUPER = 4
GROUP = 4
PICKS = 8
TIERS = (16, 32)
MESH = pl.DeviceIdType.MESH
HIGH = lax.Precision.HIGHEST
F32 = jnp.float32
BF16 = jnp.bfloat16
NT = (((1,), (1,)), ((), ()))

POS = 0
POSC = 64
ALIVE = 192
SAME = 256
POSD = 320
TARGET = 384
LEVEL = 392
PLACE = 400
COUNT = 408
DEPTH = 416
HIT = 424


def dot_nt(a, b):
    return lax.dot_general(a, b, NT, precision=HIGH, preferred_element_type=F32)


def pick_kernel(meta, a_ref, out_ref, sems):
    my_col = lax.axis_index("col")
    out_ref[...] = jnp.zeros_like(out_ref)

    def copy(p):
        slot = jnp.maximum(meta[POS + p], 0)
        target = meta[TARGET + p % PICKS]
        mine = (meta[POS + p] >= 0) & (target % 8 == my_col)
        return mine, pltpu.make_async_copy(
            a_ref.at[p // PICKS, target // 8], out_ref.at[:, slot], sems.at[slot]
        )

    @pl.loop(0, 64)
    def _(p):
        mine, c = copy(p)

        @pl.when(mine)
        def _():
            c.start()

    @pl.loop(0, 64)
    def _(p):
        mine, c = copy(p)

        @pl.when(mine)
        def _():
            c.wait()


def pick(slots, meta, blocks):
    return pl.pallas_call(
        pick_kernel,
        out_shape=jax.ShapeDtypeStruct((8, slots, 16, 128), F32),
        in_specs=[pl.BlockSpec(memory_space=pltpu.SMEM), pl.BlockSpec(memory_space=pl.ANY)],
        out_specs=pl.BlockSpec(memory_space=pltpu.VMEM),
        scratch_shapes=[pltpu.SemaphoreType.DMA((slots,))],
        compiler_params=pltpu.CompilerParams(vmem_limit_bytes=16 << 20),
        name="pick",
    )(meta, blocks)


def place():
    r = lax.axis_index("row")
    c = lax.axis_index("col")
    return r, c, c // 2, c % 2


def gather_kernel(
    dl_ref, give_ref, x_ref, d_ref, ra, acc, rb, dsrc, rr, piece,
    sa, qa, sb, qb, sc, qc, sd, qd, se, qe, sf, qf,
):
    slots = x_ref.shape[0]
    r, c, y, k = place()
    other = {"row": r, "col": y * 2 + 1 - k}

    def along(dy):
        return {"row": r, "col": lax.rem(y + dy, 4) * 2 + k}

    def across(dr):
        return {"row": lax.rem(r + dr, 16), "col": c}

    barrier = pltpu.get_barrier_semaphore()
    pl.semaphore_signal(barrier, inc=1, device_id=other, device_id_type=MESH)
    for dy in (1, 2, 3):
        pl.semaphore_signal(barrier, inc=1, device_id=along(dy), device_id_type=MESH)
    for dr in range(1, 16):
        pl.semaphore_signal(barrier, inc=1, device_id=across(dr), device_id_type=MESH)
    pl.semaphore_wait(barrier, 19)

    halves = []
    for dy in (2, 1, 3, 0):
        there = lax.rem(y + dy, 4)
        h = pltpu.make_async_remote_copy(
            src_ref=give_ref.at[there, 1 - k], dst_ref=ra.at[dy],
            send_sem=sa.at[dy], recv_sem=qa.at[dy], device_id=other, device_id_type=MESH,
        )
        h.start()
        halves.append((dy, there, h))
    quarters = []
    for dy, there, h in halves:
        h.wait_recv()
        if dy:
            acc[dy] = give_ref[there, k] + ra[dy]
            q = pltpu.make_async_remote_copy(
                src_ref=acc.at[dy], dst_ref=rb.at[dy],
                send_sem=sb.at[dy], recv_sem=qb.at[dy], device_id=along(dy), device_id_type=MESH,
            )
            q.start()
            quarters.append((dy, q))
        else:
            total = give_ref[there, k] + ra[dy]
    for dy, q in quarters:
        q.wait_recv()
        total = total + rb[dy]
    x_ref[...] = total

    for d in range(slots):
        code = dl_ref[d]
        mine = (code // 64 == r).astype(F32)
        dsrc[d * 16 : (d + 1) * 16] = x_ref[code % 64] * mine
    parts = []
    for dr in range(1, 16):
        there = lax.rem(r + dr, 16)
        h = pltpu.make_async_remote_copy(
            src_ref=dsrc.at[pl.ds(there * slots, slots)], dst_ref=rr.at[dr],
            send_sem=sc.at[dr], recv_sem=qc.at[dr], device_id=across(dr), device_id_type=MESH,
        )
        h.start()
        parts.append(h)
    total = dsrc[pl.ds(pl.multiple_of(r * slots, 8), slots)]
    for dr, h in zip(range(1, 16), parts):
        h.wait_recv()
        total = total + rr[dr]
    piece[...] = total
    mine = pl.ds(pl.multiple_of(r * slots, 8), slots)
    d_ref[y, k, mine] = total
    wholes = []
    for dr in range(1, 16):
        h = pltpu.make_async_remote_copy(
            src_ref=piece, dst_ref=d_ref.at[y, k, mine],
            send_sem=sd.at[dr], recv_sem=qd.at[dr], device_id=across(dr), device_id_type=MESH,
        )
        h.start()
        wholes.append(h)
    for h in wholes:
        h.wait_recv()
    spread(d_ref, along, other, y, k, se, qe, sf, qf)
    for _, _, h in halves:
        h.wait_send()
    for _, q in quarters:
        q.wait_send()
    for h in parts + wholes:
        h.wait_send()


def spread(ref, along, other, y, k, se, qe, sf, qf):
    outs = []
    for dy in (2, 1, 3):
        h = pltpu.make_async_remote_copy(
            src_ref=ref.at[y, k], dst_ref=ref.at[y, k],
            send_sem=se.at[dy], recv_sem=qe.at[dy], device_id=along(dy), device_id_type=MESH,
        )
        h.start()
        outs.append((dy, h))
    twins = []
    for dy in (0, 1, 3, 2):
        come = lax.rem(y + 4 - dy, 4)
        for d, h in outs:
            if d == dy:
                h.wait_recv()
        t = pltpu.make_async_remote_copy(
            src_ref=ref.at[come, k], dst_ref=ref.at[come, k],
            send_sem=sf.at[dy], recv_sem=qf.at[dy], device_id=other, device_id_type=MESH,
        )
        t.start()
        twins.append(t)
    for t in twins:
        t.wait()
    for _, h in outs:
        h.wait_send()


def gather(dl, given):
    slots = given.shape[1]
    vmem = pl.BlockSpec(memory_space=pltpu.VMEM)
    dma = pltpu.SemaphoreType.DMA
    return pl.pallas_call(
        gather_kernel,
        out_shape=(
            jax.ShapeDtypeStruct((slots, 16, 128), F32),
            jax.ShapeDtypeStruct((4, 2, slots * 16, 128), F32),
        ),
        in_specs=[pl.BlockSpec(memory_space=pltpu.SMEM), vmem],
        out_specs=(vmem, vmem),
        scratch_shapes=[
            pltpu.VMEM((4, slots, 16, 128), F32),
            pltpu.VMEM((4, slots, 16, 128), F32),
            pltpu.VMEM((4, slots, 16, 128), F32),
            pltpu.VMEM((slots * 16, 128), F32),
            pltpu.VMEM((16, slots, 128), F32),
            pltpu.VMEM((slots, 128), F32),
            dma((4,)), dma((4,)), dma((4,)), dma((4,)),
            dma((16,)), dma((16,)), dma((16,)), dma((16,)),
            dma((4,)), dma((4,)), dma((4,)), dma((4,)),
        ],
        compiler_params=pltpu.CompilerParams(
            collective_id=slots, has_side_effects=True, vmem_limit_bytes=32 << 20
        ),
        name="gather",
    )(dl, given.reshape(4, 2, slots, 16, 128))


def lane(x, i):
    return jnp.take_along_axis(x, jnp.full(x.shape, i, jnp.int32), axis=1)


def pivots(us, vs, first):
    e = {}
    for i in range(8):
        for k in range(i + 1):
            e[i, k] = lane(us[i], first + k)
    f = {}
    for k in range(8):
        f[k, k] = lax.rsqrt(e[k, k])
        for i in range(k + 1, 8):
            f[i, k] = e[i, k] * f[k, k]
        for i in range(k + 1, 8):
            for m in range(k + 1, i + 1):
                e[i, m] = e[i, m] - f[i, k] * f[m, k]
    outs, outv = [], []
    for k in range(8):
        u, v = us[k], vs[k]
        for m in range(k):
            u = u - f[k, m] * outs[m]
            v = v - f[k, m] * outv[m]
        outs.append(u * f[k, k])
        outv.append(v * f[k, k])
    return outs, outv


def split(x):
    high = x.astype(BF16)
    x = x - high.astype(F32)
    middle = x.astype(BF16)
    return high, middle, (x - middle.astype(F32)).astype(BF16)


def batched_inverse(st, ht, ub, vb, count):
    lanes = lax.broadcasted_iota(jnp.int32, (16, 128), 1)

    @pl.loop(0, 8)
    def _(c):
        base = c * 16
        us = [st[pl.ds(base + k, 8, stride=128)] for k in range(16)]
        vs = [ht[pl.ds(base + k, 8, stride=128)] for k in range(16)]
        us[:8], vs[:8] = pivots(us[:8], vs[:8], base)
        for m in range(8, 16):
            for k in range(8):
                w = lane(us[k], base + m)
                us[m] = us[m] - w * us[k]
                vs[m] = vs[m] - w * vs[k]
        us[8:], vs[8:] = pivots(us[8:], vs[8:], base + 8)
        for k in range(16):
            ht[pl.ds(base + k, 8, stride=128)] = vs[k]
            ub[pl.ds(k, 8, stride=16)] = us[k]
            vb[pl.ds(k, 8, stride=16)] = vs[k]

        @pl.when(c < 7)
        def _():
            @pl.loop(0, (count + GROUP - 1) // GROUP)
            def _(q):
                for t in range(GROUP):
                    b = q * GROUP + t
                    here = pl.ds(pl.multiple_of(b * 16, 16), 16)
                    u = ub[here]
                    x, y, z = split(jnp.where(lanes >= base + 16, u, 0.0))
                    left = jnp.concatenate([x, x, y, y, x, z], axis=0)
                    x, y, z = split(jnp.concatenate([u, vb[here]], axis=1))
                    right = jnp.concatenate([x, y, x, y, z, x], axis=0)
                    change = lax.dot_general(
                        left, right, (((0,), (0,)), ((), ())), preferred_element_type=F32
                    )
                    rows = pl.ds(pl.multiple_of(b * 128, 128), 128)
                    st[rows] -= change[:, :128]
                    ht[rows] -= change[:, 128:]


def factor_kernel(meta, x_ref, d_ref, out_ref, st, ht, ub, vb, g, f, s, w, ld):
    def same(i, j):
        return meta[SAME + i * PICKS + j] > 0

    def held(value, i, j):
        return jnp.where(i // SUPER < j // SUPER, value.astype(BF16).astype(F32), value)

    def block(i, j):
        return d_ref[:, meta[POSD + i * PICKS + j]].reshape(128, 128)

    st[...] = jnp.zeros_like(st)
    unit = lax.broadcasted_iota(jnp.int32, (128, 128), 0) == lax.broadcasted_iota(
        jnp.int32, (128, 128), 1
    )

    @pl.loop(0, meta[DEPTH])
    def _(level):
        for b in range(8):
            ht[b * 128 : (b + 1) * 128] = unit.astype(F32)

        @pl.loop(0, PICKS)
        def _(j):
            @pl.when(meta[LEVEL + j] == level)
            def _():
                s[...] = block(j, j)

                @pl.loop(0, j)
                def _(i):
                    @pl.when(same(j, i))
                    def _():
                        w[...] = block(j, i)

                        @pl.loop(0, i)
                        def _(m):
                            @pl.when(same(j, m))
                            def _():
                                w[...] -= dot_nt(
                                    held(f[j * PICKS + m], m, i), held(f[i * PICKS + m], m, i)
                                )

                        done = dot_nt(w[...], g[i])
                        f[j * PICKS + i] = done
                        done = held(done, i, j)
                        s[...] -= dot_nt(done, done)

                st[pl.ds(pl.multiple_of(meta[PLACE + j] * 128, 128), 128)] = s[...]

        batched_inverse(st, ht, ub, vb, meta[COUNT + level])

        @pl.loop(0, PICKS)
        def _(j):
            @pl.when(meta[LEVEL + j] == level)
            def _():
                g[j] = ht[pl.ds(pl.multiple_of(meta[PLACE + j] * 128, 128), 128)]

    ld[...] = jnp.zeros_like(ld)
    out_ref[...] = jnp.zeros_like(out_ref)

    @pl.loop(0, 64)
    def _(p):
        @pl.when(meta[POS + p] >= 0)
        def _():
            a = pl.multiple_of(p // PICKS * 16, 16)
            ld[p % PICKS, pl.ds(a, 16)] = x_ref[meta[POS + p]]

    @pl.loop(0, PICKS)
    def _(j):
        @pl.loop(0, j)
        def _(i):
            @pl.when(same(j, i))
            def _():
                ld[j] -= dot_nt(held(ld[i], i, j), held(f[j * PICKS + i], i, j))

        ld[j] = dot_nt(ld[j], g[j])

    @pl.loop(0, 64)
    def _(p):
        @pl.when((meta[POS + p] >= 0) & (meta[ALIVE + p] > 0))
        def _():
            a = pl.multiple_of(p // PICKS * 16, 16)
            out_ref[meta[POS + p]] = ld[p % PICKS, pl.ds(a, 16)].astype(BF16)


def factor(meta, x, d):
    slots = x.shape[0]
    vmem = pl.BlockSpec(memory_space=pltpu.VMEM)
    return pl.pallas_call(
        factor_kernel,
        out_shape=jax.ShapeDtypeStruct((slots, 16, 128), BF16),
        in_specs=[pl.BlockSpec(memory_space=pltpu.SMEM), vmem, vmem],
        out_specs=vmem,
        scratch_shapes=[
            pltpu.VMEM((1024, 128), F32),
            pltpu.VMEM((1024, 128), F32),
            pltpu.VMEM((128, 128), F32),
            pltpu.VMEM((128, 128), F32),
            pltpu.VMEM((8, 128, 128), F32),
            pltpu.VMEM((64, 128, 128), F32),
            pltpu.VMEM((128, 128), F32),
            pltpu.VMEM((128, 128), F32),
            pltpu.VMEM((8, 128, 128), F32),
        ],
        compiler_params=pltpu.CompilerParams(vmem_limit_bytes=32 << 20),
        name="factor",
    )(meta, x, d.reshape(8, slots, 16, 128))


def share_kernel(l_ref, row_ref, col_ref, se, qe, sf, qf, sg, qg, sx, qx, sz, qz):
    n = l_ref.shape[0] // 16
    r, c, y, k = place()
    z, x = r // 4, lax.rem(r, 4)
    other = {"row": r, "col": y * 2 + 1 - k}
    goal = lax.rem(r, 8)
    high = r // 8

    def along(dy):
        return {"row": r, "col": lax.rem(y + dy, 4) * 2 + k}

    def along_x(d):
        return {"row": z * 4 + lax.rem(x + d, 4), "col": c}

    def along_z(d):
        return {"row": lax.rem(z + d, 4) * 4 + x, "col": c}

    def greet(device):
        pl.semaphore_signal(barrier, inc=1, device_id=device, device_id_type=MESH)

    barrier = pltpu.get_barrier_semaphore()
    greet(other)
    for d in (1, 2, 3):
        greet(along(d))
        greet(along_x(d))
        greet(along_z(d))
    for q in range(16):
        source = c + (q // 8) * 8
        far = jnp.logical_not((source == r) & (q % 8 == c))

        @pl.when(far)
        def _():
            greet({"row": source, "col": q % 8})

    pl.semaphore_wait(barrier, 25 + jnp.where(goal == c, 0, 1))

    def send(d):
        m = lax.rem(r + d, 16)
        return pltpu.make_async_remote_copy(
            src_ref=l_ref.at[pl.ds(m * n, n)],
            dst_ref=col_ref.at[high, m // 4, lax.rem(m, 4), :, c],
            send_sem=sg.at[d], recv_sem=qg.at[high * 8 + c],
            device_id={"row": m, "col": goal}, device_id_type=MESH,
        )

    for d in range(1, 16):
        send(d).start()

    @pl.when(goal == c)
    def _():
        col_ref[high, z, x, :, c] = l_ref[pl.ds(r * n, n)]

    @pl.when(goal != c)
    def _():
        send(0).start()

    row_ref[y, k] = l_ref[...]
    outs = []
    for d in (2, 1, 3):
        h = pltpu.make_async_remote_copy(
            src_ref=row_ref.at[y, k], dst_ref=row_ref.at[y, k],
            send_sem=se.at[d], recv_sem=qe.at[d], device_id=along(d), device_id_type=MESH,
        )
        h.start()
        outs.append((d, h))

    def move(ref, s, q, device):
        h = pltpu.make_async_remote_copy(
            src_ref=ref, dst_ref=ref, send_sem=s, recv_sem=q, device_id=device, device_id_type=MESH
        )
        h.start()
        return h

    near = []
    for half in range(2):
        for q in range(half * 8, half * 8 + 8):
            far = jnp.logical_not((c + half * 8 == r) & (q % 8 == c))

            @pl.when(far)
            def _():
                pltpu.make_async_remote_copy(
                    src_ref=l_ref.at[pl.ds(0, n)], dst_ref=col_ref.at[half, z, x, :, q % 8],
                    send_sem=sg.at[0], recv_sem=qg.at[q], device_id=other, device_id_type=MESH,
                ).wait_recv()

        for d in (2, 1, 3):
            if half == 0:
                near.append(move(col_ref.at[0, z, x], sx.at[d], qx.at[d], along_x(d)))
            else:
                near.append(move(col_ref.at[1, z, x], sz.at[d], qz.at[d], along_z(d)))

    twins = []
    for d in (0, 1, 3, 2):
        come = lax.rem(y + 4 - d, 4)
        for e, h in outs:
            if e == d:
                h.wait_recv()
        twins.append(move(row_ref.at[come, k], sf.at[d], qf.at[d], other))

    for h in near:
        h.wait_recv()
    last = []
    for d in (2, 1, 3):
        last.append(move(col_ref.at[0, z], sx.at[3 + d], qx.at[3 + d], along_z(d)))
        last.append(move(col_ref.at[1, :, x], sz.at[3 + d], qz.at[3 + d], along_x(d)))
    for h in twins + last:
        h.wait()
    for h in near + [h for _, h in outs]:
        h.wait_send()
    for d in range(1, 16):
        send(d).wait_send()

    @pl.when(goal != c)
    def _():
        send(0).wait_send()


def share(l):
    slots = l.shape[0]
    vmem = pl.BlockSpec(memory_space=pltpu.VMEM)
    dma = pltpu.SemaphoreType.DMA
    return pl.pallas_call(
        share_kernel,
        out_shape=(
            jax.ShapeDtypeStruct((4, 2, slots, 16, 128), BF16),
            jax.ShapeDtypeStruct((2, 4, 4, slots // 16, 8, 16, 128), BF16),
        ),
        in_specs=[vmem],
        out_specs=(vmem, vmem),
        scratch_shapes=[
            dma((4,)), dma((4,)), dma((4,)), dma((4,)), dma((16,)), dma((16,)),
            dma((7,)), dma((7,)), dma((7,)), dma((7,)),
        ],
        compiler_params=pltpu.CompilerParams(
            collective_id=slots + 1, has_side_effects=True, vmem_limit_bytes=32 << 20
        ),
        name="share",
    )(l)


def update_kernel(meta, a_ref, row_ref, col_ref, panel_ref, out_ref):
    a = pl.program_id(0)
    for j in range(PICKS):
        slot = meta[POS + a * PICKS + j]
        lanes = slice((j % SUPER) * 128, (j % SUPER + 1) * 128)

        @pl.when(slot >= 0)
        def _():
            panel_ref[j // SUPER, 0, :, lanes] = row_ref[:, slot].reshape(128, 128)

        @pl.when(slot < 0)
        def _():
            panel_ref[j // SUPER, 0, :, lanes] = jnp.zeros((128, 128), BF16)

    for b in range(16):
        hit = meta[HIT + a * 16 + b] > 0

        @pl.when(hit)
        def _():
            out_ref[0, b] = a_ref[0, b]

            @pl.loop(0, PICKS)
            def _(j):
                slot = meta[POS + a * PICKS + j]

                @pl.when(slot >= 0)
                def _():
                    left = row_ref[:, slot].reshape(128, 128)
                    down = meta[POSC + (b % 2) * 64 + (b // 2) * PICKS + j]
                    right = col_ref[b % 2, jnp.maximum(down, 0)]
                    out_ref[0, b] -= lax.dot_general(left, right, NT, preferred_element_type=F32)

        @pl.when(jnp.logical_not(hit))
        def _():
            out_ref[0, b] = jnp.zeros((128, 128), F32)


def update(meta, blocks, rows, cols):
    slots = rows.shape[2]
    whole = lambda n: (lambda a, m: (0,) * n)
    return pl.pallas_call(
        update_kernel,
        grid_spec=pltpu.PrefetchScalarGridSpec(
            num_scalar_prefetch=1,
            grid=(8,),
            in_specs=[
                pl.BlockSpec((1, 16, 128, 128), lambda a, m: (a, 0, 0, 0)),
                pl.BlockSpec((8, slots, 16, 128), whole(4)),
                pl.BlockSpec((2, slots, 128, 128), whole(4)),
            ],
            out_specs=[
                pl.BlockSpec((2, 1, 128, 512), lambda a, m: (0, a, 0, 0)),
                pl.BlockSpec((1, 16, 128, 128), lambda a, m: (a, 0, 0, 0)),
            ],
        ),
        out_shape=(
            jax.ShapeDtypeStruct((2, 8, 128, 512), BF16),
            jax.ShapeDtypeStruct((8, 16, 128, 128), F32),
        ),
        compiler_params=pltpu.CompilerParams(vmem_limit_bytes=32 << 20),
        name="update",
    )(meta, blocks, rows.reshape(8, slots, 16, 128), cols.reshape(2, slots, 128, 128))


def tables(pattern, order, my_row, my_col):
    target = order[:PICKS]
    blocks = jnp.arange(128, dtype=jnp.int32)
    onehot = (target[:, None] == blocks[None, :]).astype(F32)
    linked = pattern.astype(F32)
    member = jnp.dot(onehot, linked)
    among = jnp.dot(member, onehot.T)
    index = jnp.arange(64, dtype=jnp.int32)
    before = (index[:, None] < index[None, :]).astype(F32)
    own = member.reshape(PICKS, 8, 16).transpose(2, 1, 0).reshape(16, 64)
    rank = jnp.dot(own, before)
    slot = jnp.where(own > 0, rank, -1.0)
    full = jnp.max(jnp.sum(own, axis=1))
    small = jnp.arange(PICKS)
    low = (small[None, :] <= small[:, None])
    ed = (among.T * low).reshape(1, 64)
    rankd = jnp.dot(ed, before)
    fulld = jnp.sum(ed)
    ed2 = ed.reshape(PICKS, PICKS)
    level = jnp.sum(ed2, axis=1).astype(jnp.int32) - 1
    peers = level[:, None] == level[None, :]
    spot = jnp.sum(peers & (small[None, :] < small[:, None]), axis=1)
    count = jnp.sum(level[None, :] == small[:, None], axis=1)
    by_block = slot.reshape(16, 8, PICKS).transpose(1, 0, 2).reshape(128, PICKS)
    where_d = jnp.dot(onehot, by_block)
    code = (target % 16)[:, None] * 64 + where_d.astype(jnp.int32)
    code = jnp.where(ed2 > 0, code, 0).reshape(64)
    rankd = jnp.where(ed > 0, rankd, -1.0).astype(jnp.int32).reshape(64)
    slots = jnp.arange(TIERS[-1], dtype=jnp.int32)
    match = rankd[None, :] == slots[:, None]
    dl = jnp.where(
        slots < fulld.astype(jnp.int32),
        jnp.sum(jnp.where(match, code[None, :], 0), axis=1),
        16 * 64,
    )
    dead = jnp.stack([jnp.sum(onehot[:SUPER], axis=0), jnp.sum(onehot, axis=0)])
    alive = 1.0 - lax.dynamic_index_in_dim(dead.reshape(2, 8, 16), my_row, 2, keepdims=False)
    alive = jnp.repeat(alive.T, SUPER, axis=1).reshape(64).astype(jnp.int32)
    slot = slot.astype(jnp.int32)
    hit = lax.dynamic_index_in_dim(pattern.reshape(8, 16, 128), my_row, 1, keepdims=False)
    hit = lax.dynamic_index_in_dim(hit.reshape(8, 16, 8), my_col, 2, keepdims=False)
    pick_row = lambda i: lax.dynamic_index_in_dim(slot, i, 0, keepdims=False)
    meta = jnp.concatenate(
        [
            pick_row(my_row), pick_row(my_col), pick_row(my_col + 8), alive,
            ed.astype(jnp.int32).reshape(64), jnp.maximum(rankd, 0),
            target, level, spot, count, jnp.full((8,), jnp.max(level) + 1), hit.reshape(128),
        ]
    ).astype(jnp.int32)
    need = jnp.maximum(full, fulld)
    tier = sum((need > slots).astype(jnp.int32) for slots in TIERS)
    return meta, dl.astype(jnp.int32), tier


def compact(slots, meta, dl, blocks):
    given = pick(slots, meta, blocks.reshape(8, 16, 8, 16, 128))
    x, d = gather(dl[:slots], given)
    l = factor(meta, x, d)
    rows, cols = share(l)
    return update(meta, blocks, rows, cols)


def broadcast(value, axis, source):
    kept = jnp.where(lax.axis_index(axis) == source, value, 0).astype(value.dtype)
    return lax.psum(kept, axis)


def dense(pattern, order, local):
    rows_axis = lax.axis_size("row")
    cols_axis = lax.axis_size("col")
    my_row = lax.axis_index("row")
    my_col = lax.axis_index("col")
    row_blocks, col_blocks, _, width = local.shape
    local = with_layout_constraint(local, Layout((0, 1, 2, 3)))
    ratio = rows_axis // cols_axis
    total_blocks = row_blocks * rows_axis
    my_pattern = lax.dynamic_index_in_dim(
        pattern.reshape(row_blocks, rows_axis, total_blocks), my_row, 1, keepdims=False
    )
    my_pattern = lax.dynamic_index_in_dim(
        my_pattern.reshape(row_blocks, col_blocks, cols_axis), my_col, 2, keepdims=False
    )
    current = local * my_pattern.astype(F32)[:, :, None, None]
    dead = jnp.zeros((total_blocks,), F32)
    results = []
    for step in range(2):
        chosen = order[step * SUPER : (step + 1) * SUPER]
        pieces = []
        for member in range(SUPER):
            target = chosen[member]
            column_here = lax.dynamic_index_in_dim(current, target // cols_axis, 1, keepdims=False)
            pieces.append(broadcast(column_here, "col", target % cols_axis))
        panel = jnp.concatenate(pieces, axis=2)
        parts_list = []
        for member in range(SUPER):
            target = chosen[member]
            row_here = lax.dynamic_index_in_dim(panel, target // rows_axis, 0, keepdims=False)
            parts_list.append(
                jnp.where(target % rows_axis == my_row, row_here, jnp.zeros_like(row_here))
            )
        square = lax.psum(jnp.concatenate(parts_list, axis=0), "row")
        factored = jnp.linalg.cholesky(square)
        flat = panel.reshape(row_blocks * width, SUPER * width)
        lower = lax.linalg.triangular_solve(
            factored, flat, left_side=False, lower=True, transpose_a=True
        )
        dead = dead.at[chosen].set(1.0)
        alive = lax.dynamic_index_in_dim(
            (1.0 - dead).reshape(row_blocks, rows_axis), my_row, 1, keepdims=False
        )
        rounded = (lower.reshape(row_blocks, width, SUPER * width) * alive[:, None, None]).astype(
            BF16
        )
        results.append(rounded)
        whole = lax.all_gather(rounded, "row", axis=0, tiled=True)
        whole = whole.reshape(ratio, cols_axis, row_blocks, width, SUPER * width)
        picked = lax.dynamic_index_in_dim(whole, my_col, 1, keepdims=False)
        column_panel = picked.transpose(1, 0, 2, 3).reshape(col_blocks, width, SUPER * width)
        change = jnp.einsum("aik,cjk->acij", rounded, column_panel, preferred_element_type=F32)
        current = current - change
    panels = with_layout_constraint(jnp.stack(results), Layout((0, 1, 2, 3)))
    return panels, with_layout_constraint(current, Layout((0, 1, 2, 3)))


def shards(matrix_blocks, pattern, order):
    local = matrix_blocks[:, 0, :, 0]
    meta, dl, tier = tables(pattern, order, lax.axis_index("row"), lax.axis_index("col"))
    ways = [functools.partial(compact, slots, meta, dl, local) for slots in TIERS]
    panels, trailing = lax.switch(tier, ways + [lambda: dense(pattern, order, local)])
    return panels[:, :, None], trailing[:, None, :, None]


def solution(mesh):
    in_specs = (P(None, "row", None, "col", None, None), P(), P())
    out_specs = (P(None, None, "row", None, None), P(None, "row", None, "col", None, None))
    return jax.shard_map(shards, mesh=mesh, in_specs=in_specs, out_specs=out_specs, check_vma=False)
```

```python
import functools

import jax
import jax.numpy as jnp
from jax import lax
from jax.experimental import pallas as pl
from jax.experimental.pallas import tpu as pltpu
from jax.sharding import PartitionSpec as P

SUPER = 4
GROUP = 4
PICKS = 8
TIERS = (16, 32, 64)
MESH = pl.DeviceIdType.MESH
HIGH = lax.Precision.HIGHEST
F32 = jnp.float32
BF16 = jnp.bfloat16
NT = (((1,), (1,)), ((), ()))

LABEL = 8
ELIM = 9
TARGET = 10
LEVEL = 11
SPOT = 12
COUNT = 13
SOURCE = 14
SIZES = 15
SLOTD = 16


def dot_nt(a, b):
    return lax.dot_general(a, b, NT, precision=HIGH, preferred_element_type=F32)


def pick_kernel(meta, a_ref, out_ref, sems):
    my_row = lax.axis_index("row")
    my_col = lax.axis_index("col")
    out_ref[...] = jnp.zeros_like(out_ref)

    def copy(p):
        slot = meta[p % PICKS, p // PICKS * 16 + my_row]
        target = meta[TARGET, p % PICKS]
        mine = (slot >= 0) & (target % 8 == my_col)
        slot = jnp.maximum(slot, 0)
        return mine, pltpu.make_async_copy(
            a_ref.at[p // PICKS, target // 8], out_ref.at[:, slot], sems.at[slot]
        )

    @pl.loop(0, 64)
    def _(p):
        mine, c = copy(p)

        @pl.when(mine)
        def _():
            c.start()

    @pl.loop(0, 64)
    def _(p):
        mine, c = copy(p)

        @pl.when(mine)
        def _():
            c.wait()


def pick(slots, meta, blocks):
    return pl.pallas_call(
        pick_kernel,
        out_shape=jax.ShapeDtypeStruct((8, slots, 16, 128), F32),
        in_specs=[pl.BlockSpec(memory_space=pltpu.SMEM), pl.BlockSpec(memory_space=pl.ANY)],
        out_specs=pl.BlockSpec(memory_space=pltpu.VMEM),
        scratch_shapes=[pltpu.SemaphoreType.DMA((slots,))],
        compiler_params=pltpu.CompilerParams(vmem_limit_bytes=24 << 20),
        name="pick",
    )(meta, blocks)


def place():
    r = lax.axis_index("row")
    c = lax.axis_index("col")
    return r, c, c // 2, c % 2


def gather_kernel(
    meta, give_ref, x_ref, d_ref, ra, acc, rb, dsrc, rr, piece,
    sa, qa, sb, qb, sc, qc, sd, qd, se, qe, sf, qf,
):
    slots = x_ref.shape[0]
    r, c, y, k = place()
    other = {"row": r, "col": y * 2 + 1 - k}

    def along(dy):
        return {"row": r, "col": lax.rem(y + dy, 4) * 2 + k}

    def across(dr):
        return {"row": lax.rem(r + dr, 16), "col": c}

    barrier = pltpu.get_barrier_semaphore()
    pl.semaphore_signal(barrier, inc=1, device_id=other, device_id_type=MESH)
    for dy in (1, 2, 3):
        pl.semaphore_signal(barrier, inc=1, device_id=along(dy), device_id_type=MESH)
    for dr in range(1, 16):
        pl.semaphore_signal(barrier, inc=1, device_id=across(dr), device_id_type=MESH)
    pl.semaphore_wait(barrier, 19)

    halves = []
    for dy in (2, 1, 3, 0):
        there = lax.rem(y + dy, 4)
        h = pltpu.make_async_remote_copy(
            src_ref=give_ref.at[there, 1 - k], dst_ref=ra.at[dy],
            send_sem=sa.at[dy], recv_sem=qa.at[dy], device_id=other, device_id_type=MESH,
        )
        h.start()
        halves.append((dy, there, h))
    quarters = []
    for dy, there, h in halves:
        h.wait_recv()
        if dy:
            acc[dy] = give_ref[there, k] + ra[dy]
            q = pltpu.make_async_remote_copy(
                src_ref=acc.at[dy], dst_ref=rb.at[dy],
                send_sem=sb.at[dy], recv_sem=qb.at[dy], device_id=along(dy), device_id_type=MESH,
            )
            q.start()
            quarters.append((dy, q))
        else:
            total = give_ref[there, k] + ra[dy]
    for dy, q in quarters:
        q.wait_recv()
        total = total + rb[dy]
    x_ref[...] = total

    for d in range(slots):
        code = meta[SOURCE, d]
        mine = (code // 64 == r).astype(F32)
        dsrc[d * 16 : (d + 1) * 16] = x_ref[code % 64] * mine
    parts = []
    for dr in range(1, 16):
        there = lax.rem(r + dr, 16)
        h = pltpu.make_async_remote_copy(
            src_ref=dsrc.at[pl.ds(there * slots, slots)], dst_ref=rr.at[dr],
            send_sem=sc.at[dr], recv_sem=qc.at[dr], device_id=across(dr), device_id_type=MESH,
        )
        h.start()
        parts.append(h)
    total = dsrc[pl.ds(pl.multiple_of(r * slots, 8), slots)]
    for dr, h in zip(range(1, 16), parts):
        h.wait_recv()
        total = total + rr[dr]
    piece[...] = total
    mine = pl.ds(pl.multiple_of(r * slots, 8), slots)
    d_ref[y, k, mine] = total
    wholes = []
    for dr in range(1, 16):
        h = pltpu.make_async_remote_copy(
            src_ref=piece, dst_ref=d_ref.at[y, k, mine],
            send_sem=sd.at[dr], recv_sem=qd.at[dr], device_id=across(dr), device_id_type=MESH,
        )
        h.start()
        wholes.append(h)
    for h in wholes:
        h.wait_recv()
    spread(d_ref, along, other, y, k, se, qe, sf, qf)
    for _, _, h in halves:
        h.wait_send()
    for _, q in quarters:
        q.wait_send()
    for h in parts + wholes:
        h.wait_send()


def spread(ref, along, other, y, k, se, qe, sf, qf):
    outs = []
    for dy in (2, 1, 3):
        h = pltpu.make_async_remote_copy(
            src_ref=ref.at[y, k], dst_ref=ref.at[y, k],
            send_sem=se.at[dy], recv_sem=qe.at[dy], device_id=along(dy), device_id_type=MESH,
        )
        h.start()
        outs.append((dy, h))
    twins = []
    for dy in (0, 1, 3, 2):
        come = lax.rem(y + 4 - dy, 4)
        for d, h in outs:
            if d == dy:
                h.wait_recv()
        t = pltpu.make_async_remote_copy(
            src_ref=ref.at[come, k], dst_ref=ref.at[come, k],
            send_sem=sf.at[dy], recv_sem=qf.at[dy], device_id=other, device_id_type=MESH,
        )
        t.start()
        twins.append(t)
    for t in twins:
        t.wait()
    for _, h in outs:
        h.wait_send()


def gather(meta, given):
    slots = given.shape[1]
    vmem = pl.BlockSpec(memory_space=pltpu.VMEM)
    dma = pltpu.SemaphoreType.DMA
    return pl.pallas_call(
        gather_kernel,
        out_shape=(
            jax.ShapeDtypeStruct((slots, 16, 128), F32),
            jax.ShapeDtypeStruct((4, 2, slots * 16, 128), F32),
        ),
        in_specs=[pl.BlockSpec(memory_space=pltpu.SMEM), vmem],
        out_specs=(vmem, vmem),
        scratch_shapes=[
            pltpu.VMEM((4, slots, 16, 128), F32),
            pltpu.VMEM((4, slots, 16, 128), F32),
            pltpu.VMEM((4, slots, 16, 128), F32),
            pltpu.VMEM((slots * 16, 128), F32),
            pltpu.VMEM((16, slots, 128), F32),
            pltpu.VMEM((slots, 128), F32),
            dma((4,)), dma((4,)), dma((4,)), dma((4,)),
            dma((16,)), dma((16,)), dma((16,)), dma((16,)),
            dma((4,)), dma((4,)), dma((4,)), dma((4,)),
        ],
        compiler_params=pltpu.CompilerParams(
            collective_id=slots, has_side_effects=True, vmem_limit_bytes=48 << 20
        ),
        name="gather",
    )(meta, given.reshape(4, 2, slots, 16, 128))


def lane(x, i):
    return jnp.take_along_axis(x, jnp.full(x.shape, i, jnp.int32), axis=1)


def pivots(us, vs, first):
    e = {}
    for i in range(8):
        for k in range(i + 1):
            e[i, k] = lane(us[i], first + k)
    f = {}
    for k in range(8):
        f[k, k] = lax.rsqrt(e[k, k])
        for i in range(k + 1, 8):
            f[i, k] = e[i, k] * f[k, k]
        for i in range(k + 1, 8):
            for m in range(k + 1, i + 1):
                e[i, m] = e[i, m] - f[i, k] * f[m, k]
    outs, outv = [], []
    for k in range(8):
        u, v = us[k], vs[k]
        for m in range(k):
            u = u - f[k, m] * outs[m]
            v = v - f[k, m] * outv[m]
        outs.append(u * f[k, k])
        outv.append(v * f[k, k])
    return outs, outv


def split(x):
    high = x.astype(BF16)
    x = x - high.astype(F32)
    middle = x.astype(BF16)
    return high, middle, (x - middle.astype(F32)).astype(BF16)


def batched_inverse(st, ht, ub, vb, count):
    lanes = lax.broadcasted_iota(jnp.int32, (16, 128), 1)

    @pl.loop(0, 8)
    def _(c):
        base = c * 16
        us = [st[pl.ds(base + k, 8, stride=128)] for k in range(16)]
        vs = [ht[pl.ds(base + k, 8, stride=128)] for k in range(16)]
        us[:8], vs[:8] = pivots(us[:8], vs[:8], base)
        for m in range(8, 16):
            for k in range(8):
                w = lane(us[k], base + m)
                us[m] = us[m] - w * us[k]
                vs[m] = vs[m] - w * vs[k]
        us[8:], vs[8:] = pivots(us[8:], vs[8:], base + 8)
        for k in range(16):
            ht[pl.ds(base + k, 8, stride=128)] = vs[k]
            ub[pl.ds(k, 8, stride=16)] = us[k]
            vb[pl.ds(k, 8, stride=16)] = vs[k]

        @pl.when(c < 7)
        def _():
            @pl.loop(0, (count + GROUP - 1) // GROUP)
            def _(q):
                for t in range(GROUP):
                    b = q * GROUP + t
                    here = pl.ds(pl.multiple_of(b * 16, 16), 16)
                    u = ub[here]
                    x, y, z = split(jnp.where(lanes >= base + 16, u, 0.0))
                    left = jnp.concatenate([x, x, y, y, x, z], axis=0)
                    x, y, z = split(jnp.concatenate([u, vb[here]], axis=1))
                    right = jnp.concatenate([x, y, x, y, z, x], axis=0)
                    change = lax.dot_general(
                        left, right, (((0,), (0,)), ((), ())), preferred_element_type=F32
                    )
                    rows = pl.ds(pl.multiple_of(b * 128, 128), 128)
                    st[rows] -= change[:, :128]
                    ht[rows] -= change[:, 128:]


def factor_kernel(meta, x_ref, d_ref, out_ref, st, ht, ub, vb, g, f, s, w, ld, lf):
    def same(i, j):
        return meta[SLOTD + i, j] >= 0

    def held(value, i, j):
        return jnp.where(i // SUPER < j // SUPER, value.astype(BF16).astype(F32), value)

    def block(i, j):
        return d_ref[:, meta[SLOTD + i, j]].reshape(128, 128)

    st[...] = jnp.zeros_like(st)
    unit = lax.broadcasted_iota(jnp.int32, (128, 128), 0) == lax.broadcasted_iota(
        jnp.int32, (128, 128), 1
    )

    @pl.loop(0, meta[SIZES, 1])
    def _(level):
        for b in range(8):
            ht[b * 128 : (b + 1) * 128] = unit.astype(F32)

        @pl.loop(0, PICKS)
        def _(j):
            @pl.when(meta[LEVEL, j] == level)
            def _():
                s[...] = block(j, j)

                @pl.loop(0, j)
                def _(i):
                    @pl.when(same(j, i))
                    def _():
                        w[...] = block(j, i)

                        @pl.loop(0, i)
                        def _(m):
                            @pl.when(same(j, m))
                            def _():
                                w[...] -= dot_nt(
                                    held(f[j * PICKS + m], m, i), held(f[i * PICKS + m], m, i)
                                )

                        done = dot_nt(w[...], g[i])
                        f[j * PICKS + i] = done
                        done = held(done, i, j)
                        s[...] -= dot_nt(done, done)

                st[pl.ds(pl.multiple_of(meta[SPOT, j] * 128, 128), 128)] = s[...]

        batched_inverse(st, ht, ub, vb, meta[COUNT, level])

        @pl.loop(0, PICKS)
        def _(j):
            @pl.when(meta[LEVEL, j] == level)
            def _():
                g[j] = ht[pl.ds(pl.multiple_of(meta[SPOT, j] * 128, 128), 128)]

    my_row = lax.axis_index("row")
    ld[...] = jnp.zeros_like(ld)
    out_ref[...] = jnp.zeros_like(out_ref)

    @pl.loop(0, 64)
    def _(p):
        slot = meta[p % PICKS, p // PICKS * 16 + my_row]

        @pl.when(slot >= 0)
        def _():
            a = pl.multiple_of(p // PICKS * 16, 16)
            ld[p % PICKS, pl.ds(a, 16)] = x_ref[slot]

    for j in range(PICKS):
        lf[j] = dot_nt(ld[j], g[j])

    @pl.loop(1, PICKS)
    def _(j):
        @pl.when(meta[LEVEL, j] > 0)
        def _():
            @pl.loop(0, j)
            def _(i):
                @pl.when(same(j, i))
                def _():
                    ld[j] -= dot_nt(held(lf[i], i, j), held(f[j * PICKS + i], i, j))

            lf[j] = dot_nt(ld[j], g[j])

    @pl.loop(0, 64)
    def _(p):
        here = p // PICKS * 16 + my_row
        slot = meta[p % PICKS, here]
        elim = meta[ELIM, here]
        alive = (elim < 0) | (elim >= (p % PICKS // SUPER + 1) * SUPER)

        @pl.when((slot >= 0) & alive)
        def _():
            a = pl.multiple_of(p // PICKS * 16, 16)
            out_ref[slot] = lf[p % PICKS, pl.ds(a, 16)].astype(BF16)


def factor(meta, x, d):
    slots = x.shape[0]
    vmem = pl.BlockSpec(memory_space=pltpu.VMEM)
    return pl.pallas_call(
        factor_kernel,
        out_shape=jax.ShapeDtypeStruct((slots, 16, 128), BF16),
        in_specs=[pl.BlockSpec(memory_space=pltpu.SMEM), vmem, vmem],
        out_specs=vmem,
        scratch_shapes=[
            pltpu.VMEM((1024, 128), F32),
            pltpu.VMEM((1024, 128), F32),
            pltpu.VMEM((128, 128), F32),
            pltpu.VMEM((128, 128), F32),
            pltpu.VMEM((8, 128, 128), F32),
            pltpu.VMEM((64, 128, 128), F32),
            pltpu.VMEM((128, 128), F32),
            pltpu.VMEM((128, 128), F32),
            pltpu.VMEM((8, 128, 128), F32),
            pltpu.VMEM((8, 128, 128), F32),
        ],
        compiler_params=pltpu.CompilerParams(vmem_limit_bytes=48 << 20),
        name="factor",
    )(meta, x, d.reshape(8, slots, 16, 128))


def share_kernel(l_ref, row_ref, col_ref, se, qe, sf, qf, sg, qg, sx, qx, sz, qz):
    n = l_ref.shape[0] // 16
    r, c, y, k = place()
    z, x = r // 4, lax.rem(r, 4)
    other = {"row": r, "col": y * 2 + 1 - k}
    goal = lax.rem(r, 8)
    high = r // 8

    def along(dy):
        return {"row": r, "col": lax.rem(y + dy, 4) * 2 + k}

    def along_x(d):
        return {"row": z * 4 + lax.rem(x + d, 4), "col": c}

    def along_z(d):
        return {"row": lax.rem(z + d, 4) * 4 + x, "col": c}

    def greet(device):
        pl.semaphore_signal(barrier, inc=1, device_id=device, device_id_type=MESH)

    barrier = pltpu.get_barrier_semaphore()
    greet(other)
    for d in (1, 2, 3):
        greet(along(d))
        greet(along_x(d))
        greet(along_z(d))
    for q in range(16):
        source = c + (q // 8) * 8
        far = jnp.logical_not((source == r) & (q % 8 == c))

        @pl.when(far)
        def _():
            greet({"row": source, "col": q % 8})

    pl.semaphore_wait(barrier, 25 + jnp.where(goal == c, 0, 1))

    def send(d):
        m = lax.rem(r + d, 16)
        return pltpu.make_async_remote_copy(
            src_ref=l_ref.at[pl.ds(m * n, n)],
            dst_ref=col_ref.at[high, m // 4, lax.rem(m, 4), :, c],
            send_sem=sg.at[d], recv_sem=qg.at[high * 8 + c],
            device_id={"row": m, "col": goal}, device_id_type=MESH,
        )

    for d in range(1, 16):
        send(d).start()

    @pl.when(goal == c)
    def _():
        col_ref[high, z, x, :, c] = l_ref[pl.ds(r * n, n)]

    @pl.when(goal != c)
    def _():
        send(0).start()

    row_ref[y, k] = l_ref[...]
    outs = []
    for d in (2, 1, 3):
        h = pltpu.make_async_remote_copy(
            src_ref=row_ref.at[y, k], dst_ref=row_ref.at[y, k],
            send_sem=se.at[d], recv_sem=qe.at[d], device_id=along(d), device_id_type=MESH,
        )
        h.start()
        outs.append((d, h))

    def move(ref, s, q, device):
        h = pltpu.make_async_remote_copy(
            src_ref=ref, dst_ref=ref, send_sem=s, recv_sem=q, device_id=device, device_id_type=MESH
        )
        h.start()
        return h

    near = []
    for half in range(2):
        for q in range(half * 8, half * 8 + 8):
            far = jnp.logical_not((c + half * 8 == r) & (q % 8 == c))

            @pl.when(far)
            def _():
                pltpu.make_async_remote_copy(
                    src_ref=l_ref.at[pl.ds(0, n)], dst_ref=col_ref.at[half, z, x, :, q % 8],
                    send_sem=sg.at[0], recv_sem=qg.at[q], device_id=other, device_id_type=MESH,
                ).wait_recv()

        for d in (2, 1, 3):
            if half == 0:
                near.append(move(col_ref.at[0, z, x], sx.at[d], qx.at[d], along_x(d)))
            else:
                near.append(move(col_ref.at[1, z, x], sz.at[d], qz.at[d], along_z(d)))

    twins = []
    for d in (0, 1, 3, 2):
        come = lax.rem(y + 4 - d, 4)
        for e, h in outs:
            if e == d:
                h.wait_recv()
        twins.append(move(row_ref.at[come, k], sf.at[d], qf.at[d], other))

    for h in near:
        h.wait_recv()
    last = []
    for d in (2, 1, 3):
        last.append(move(col_ref.at[0, z], sx.at[3 + d], qx.at[3 + d], along_z(d)))
        last.append(move(col_ref.at[1, :, x], sz.at[3 + d], qz.at[3 + d], along_x(d)))
    for h in twins + last:
        h.wait()
    for h in near + [h for _, h in outs]:
        h.wait_send()
    for d in range(1, 16):
        send(d).wait_send()

    @pl.when(goal != c)
    def _():
        send(0).wait_send()


def share(l):
    slots = l.shape[0]
    vmem = pl.BlockSpec(memory_space=pltpu.VMEM)
    dma = pltpu.SemaphoreType.DMA
    return pl.pallas_call(
        share_kernel,
        out_shape=(
            jax.ShapeDtypeStruct((4, 2, slots, 16, 128), BF16),
            jax.ShapeDtypeStruct((2, 4, 4, slots // 16, 8, 16, 128), BF16),
        ),
        in_specs=[vmem],
        out_specs=(vmem, vmem),
        scratch_shapes=[
            dma((4,)), dma((4,)), dma((4,)), dma((4,)), dma((16,)), dma((16,)),
            dma((7,)), dma((7,)), dma((7,)), dma((7,)),
        ],
        compiler_params=pltpu.CompilerParams(
            collective_id=slots + 1, has_side_effects=True, vmem_limit_bytes=48 << 20
        ),
        name="share",
    )(l)


def update_kernel(meta, a_ref, row_ref, col_ref, panel_ref, out_ref):
    a = pl.program_id(0)
    my_col = lax.axis_index("col")
    g = a * 16 + lax.axis_index("row")
    for j in range(PICKS):
        slot = meta[j, g]
        lanes = slice((j % SUPER) * 128, (j % SUPER + 1) * 128)

        @pl.when(slot >= 0)
        def _():
            panel_ref[j // SUPER, 0, :, lanes] = row_ref[:, slot].reshape(128, 128)

        @pl.when(slot < 0)
        def _():
            panel_ref[j // SUPER, 0, :, lanes] = jnp.zeros((128, 128), BF16)

    for b in range(16):
        h = b * 8 + my_col
        hit = meta[LABEL, g] == meta[LABEL, h]

        @pl.when(hit)
        def _():
            out_ref[0, b] = a_ref[0, b]

            @pl.loop(0, PICKS)
            def _(j):
                slot = meta[j, g]

                @pl.when(slot >= 0)
                def _():
                    left = row_ref[:, slot].reshape(128, 128)
                    right = col_ref[b % 2, jnp.maximum(meta[j, h], 0)]
                    out_ref[0, b] -= lax.dot_general(left, right, NT, preferred_element_type=F32)

        @pl.when(jnp.logical_not(hit))
        def _():
            out_ref[0, b] = jnp.zeros((128, 128), F32)


def update(meta, blocks, rows, cols):
    slots = rows.shape[2]
    whole = lambda n: (lambda a, m: (0,) * n)
    return pl.pallas_call(
        update_kernel,
        grid_spec=pltpu.PrefetchScalarGridSpec(
            num_scalar_prefetch=1,
            grid=(8,),
            in_specs=[
                pl.BlockSpec((1, 16, 128, 128), lambda a, m: (a, 0, 0, 0)),
                pl.BlockSpec((8, slots, 16, 128), whole(4)),
                pl.BlockSpec((2, slots, 128, 128), whole(4)),
            ],
            out_specs=[
                pl.BlockSpec((2, 1, 128, 512), lambda a, m: (0, a, 0, 0)),
                pl.BlockSpec((1, 16, 128, 128), lambda a, m: (a, 0, 0, 0)),
            ],
        ),
        out_shape=(
            jax.ShapeDtypeStruct((2, 8, 128, 512), BF16),
            jax.ShapeDtypeStruct((8, 16, 128, 128), F32),
        ),
        compiler_params=pltpu.CompilerParams(vmem_limit_bytes=48 << 20),
        name="update",
    )(meta, blocks, rows.reshape(8, slots, 16, 128), cols.reshape(2, slots, 128, 128))


def ranks(marks, before):
    total = jnp.sum(marks, axis=0, keepdims=True)
    run = jnp.dot(jnp.broadcast_to(total, (8, 128)), before, preferred_element_type=F32)[:1]
    rows = []
    for j in range(8):
        rows.append(jnp.where(marks[j : j + 1] > 0, run, -1.0))
        run = run + marks[j : j + 1]
    return jnp.concatenate(rows, axis=0), jnp.max(run, axis=1, keepdims=True)


def tables_kernel(order, pattern_ref, meta_ref):
    lanes = lax.broadcasted_iota(jnp.int32, (8, 128), 1)
    rows = lax.broadcasted_iota(jnp.int32, (8, 128), 0)
    lane = lanes[:1]
    g = lax.broadcasted_iota(jnp.int32, (128, 128), 0)
    h = lax.broadcasted_iota(jnp.int32, (128, 128), 1)
    onehot = jnp.zeros((8, 128), F32)
    target = jnp.zeros((1, 128), jnp.int32)
    for j in range(PICKS):
        onehot = jnp.where((rows == j) & (lanes == order[j]), 1.0, onehot)
        target = jnp.where(lane == j, order[j], target)
    linked = pattern_ref[...].astype(F32)
    pad = lambda x: jnp.concatenate([x, jnp.zeros((120, 128), F32)], axis=0)
    small = lambda a, b: lax.dot_general(a, b, NT, preferred_element_type=F32)
    member = jnp.dot(onehot, linked, preferred_element_type=F32)
    slot, full = ranks(member, (((g & 15) == (h & 15)) & (g < h)).astype(F32))
    among = small(onehot, pad(member))
    lower = jnp.where(lanes <= rows, among, 0.0)
    upper = jnp.where(rows <= lanes, among, 0.0)
    slotd, fulld = ranks(lower, (g < h).astype(F32))
    home = jnp.sum(onehot * (lanes & 15).astype(F32), axis=1, keepdims=True)
    code = home * 64.0 + small(onehot, pad(slot))
    source = jnp.zeros((8, 128), F32)
    for j in range(PICKS):
        source = source + jnp.where(slotd[:, j : j + 1] == lanes.astype(F32), code[:, j : j + 1], 0.0)
    source = jnp.sum(source, axis=0, keepdims=True)
    source = jnp.where(lane.astype(F32) < fulld, source, 1024.0)
    down = jnp.sum(lower, axis=1, keepdims=True) - 1.0
    level = jnp.sum(upper, axis=0, keepdims=True) - 1.0
    spot = jnp.sum(jnp.where((down == level) & (rows < lanes), 1.0, 0.0), axis=0, keepdims=True)
    count = jnp.sum(jnp.where(down == lanes.astype(F32), 1.0, 0.0), axis=0, keepdims=True)
    depth = jnp.max(down, axis=0, keepdims=True) + 1.0
    sizes = jnp.where(lane == 0, jnp.maximum(full, fulld), depth)
    elim = jnp.sum(onehot * (rows + 1).astype(F32), axis=0, keepdims=True) - 1.0
    label = jnp.min(jnp.where(linked > 0, g.astype(F32), 999.0), axis=0, keepdims=True)

    def put(row, value):
        meta_ref[row : row + value.shape[0]] = value.astype(jnp.int32)

    put(0, slot)
    put(LABEL, label)
    put(ELIM, elim)
    put(TARGET, target)
    put(LEVEL, level)
    put(SPOT, spot)
    put(COUNT, count)
    put(SOURCE, source)
    put(SIZES, sizes)
    put(SLOTD, slotd)


def tables(pattern, order):
    vmem = pl.BlockSpec(memory_space=pltpu.VMEM)
    return pl.pallas_call(
        tables_kernel,
        out_shape=jax.ShapeDtypeStruct((24, 128), jnp.int32),
        in_specs=[pl.BlockSpec(memory_space=pltpu.SMEM), vmem],
        out_specs=vmem,
        name="tables",
    )(order, pattern)


def compact(slots, meta, blocks):
    given = pick(slots, meta, blocks.reshape(8, 16, 8, 16, 128))
    x, d = gather(meta, given)
    l = factor(meta, x, d)
    rows, cols = share(l)
    return update(meta, blocks, rows, cols)


def shards(matrix_blocks, pattern, order):
    local = matrix_blocks[:, 0, :, 0]
    meta = tables(pattern, order)
    tier = sum((meta[SIZES, 0] > slots).astype(jnp.int32) for slots in TIERS[:-1])
    ways = [functools.partial(compact, slots, meta, local) for slots in TIERS]
    panels, trailing = lax.switch(tier, ways)
    return panels[:, :, None], trailing[:, None, :, None]


def solution(mesh):
    in_specs = (P(None, "row", None, "col", None, None), P(), P())
    out_specs = (P(None, None, "row", None, None), P(None, "row", None, "col", None, None))
    return jax.shard_map(shards, mesh=mesh, in_specs=in_specs, out_specs=out_specs, check_vma=False)
```

```python
import functools

import jax
import jax.numpy as jnp
from jax import lax
from jax.experimental import pallas as pl
from jax.experimental.pallas import tpu as pltpu
from jax.sharding import PartitionSpec as P

SUPER = 4
GROUP = 4
AHEAD = 4
PICKS = 8
TIERS = (16, 32, 64)
MESH = pl.DeviceIdType.MESH
HIGH = lax.Precision.HIGHEST
F32 = jnp.float32
BF16 = jnp.bfloat16
NT = (((1,), (1,)), ((), ()))

LABEL = 8
ELIM = 9
TARGET = 10
LEVEL = 11
SPOT = 12
COUNT = 13
SOURCE = 14
SIZES = 15
NUMBER = 24
ONE = 25
TWO = 26
HITS = 27
LIST = 32
SLOTD = 16


def dot_nt(a, b):
    return lax.dot_general(a, b, NT, precision=HIGH, preferred_element_type=F32)


def pick_kernel(meta, a_ref, out_ref, sems):
    my_row = lax.axis_index("row")
    my_col = lax.axis_index("col")
    out_ref[...] = jnp.zeros_like(out_ref)

    def each(act):
        @pl.loop(0, PICKS)
        def _(j):
            target = meta[TARGET, j]

            @pl.when(target % 8 == my_col)
            def _():
                for a in range(8):
                    slot = meta[j, a * 16 + my_row]

                    @pl.when(slot >= 0)
                    def _():
                        act(
                            pltpu.make_async_copy(
                                a_ref.at[a, target // 8], out_ref.at[:, slot], sems.at[slot]
                            )
                        )

    each(lambda copy: copy.start())
    each(lambda copy: copy.wait())


def pick(slots, meta, blocks):
    return pl.pallas_call(
        pick_kernel,
        out_shape=jax.ShapeDtypeStruct((8, slots, 16, 128), F32),
        in_specs=[pl.BlockSpec(memory_space=pltpu.SMEM), pl.BlockSpec(memory_space=pl.ANY)],
        out_specs=pl.BlockSpec(memory_space=pltpu.VMEM),
        scratch_shapes=[pltpu.SemaphoreType.DMA((slots,))],
        compiler_params=pltpu.CompilerParams(vmem_limit_bytes=24 << 20),
        name="pick",
    )(meta, blocks)


def place():
    r = lax.axis_index("row")
    c = lax.axis_index("col")
    return r, c, c // 2, c % 2


def gather_kernel(
    meta, give_ref, x_ref, d_ref, ra, acc, rb, dsrc, rr, piece,
    sa, qa, sb, qb, sc, qc, sd, qd, se, qe, sf, qf,
):
    slots = x_ref.shape[0]
    r, c, y, k = place()
    other = {"row": r, "col": y * 2 + 1 - k}

    def along(dy):
        return {"row": r, "col": lax.rem(y + dy, 4) * 2 + k}

    def across(dr):
        return {"row": lax.rem(r + dr, 16), "col": c}

    z, x = r // 4, lax.rem(r, 4)

    def along_x(d):
        return {"row": z * 4 + lax.rem(x + d, 4), "col": c}

    def along_z(d):
        return {"row": lax.rem(z + d, 4) * 4 + x, "col": c}

    inside = y // 2 == k

    def to_half(dy):
        return {"row": r, "col": lax.rem(y + dy, 4) * 2 + y // 2}

    barrier = pltpu.get_barrier_semaphore()
    pl.semaphore_signal(barrier, inc=1, device_id=other, device_id_type=MESH)
    for dy in (1, 2, 3):
        pl.semaphore_signal(barrier, inc=1, device_id=along(dy), device_id_type=MESH)
    for dr in range(1, 16):
        pl.semaphore_signal(barrier, inc=1, device_id=across(dr), device_id_type=MESH)
    for q in range(4):
        @pl.when(4 * k + q != c)
        def _():
            pl.semaphore_signal(
                barrier, inc=1, device_id={"row": r, "col": 4 * k + q}, device_id_type=MESH
            )

    pl.semaphore_wait(barrier, 22 + jnp.where(inside, 0, 1))

    halves = []
    for dy in (2, 1, 3, 0):
        there = lax.rem(y + dy, 4)
        h = pltpu.make_async_remote_copy(
            src_ref=give_ref.at[there, 1 - k], dst_ref=ra.at[dy],
            send_sem=sa.at[dy], recv_sem=qa.at[dy], device_id=other, device_id_type=MESH,
        )
        h.start()
        halves.append((dy, there, h))
    quarters = []
    for dy, there, h in halves:
        h.wait_recv()
        if dy:
            acc[dy] = give_ref[there, k] + ra[dy]
            q = pltpu.make_async_remote_copy(
                src_ref=acc.at[dy], dst_ref=rb.at[dy],
                send_sem=sb.at[dy], recv_sem=qb.at[dy], device_id=along(dy), device_id_type=MESH,
            )
            q.start()
            quarters.append((dy, q))
        else:
            total = give_ref[there, k] + ra[dy]
    for dy, q in quarters:
        q.wait_recv()
        total = total + rb[dy]
    x_ref[...] = total

    for d in range(slots):
        code = meta[SOURCE, d]
        mine = (code // 64 == r).astype(F32)
        dsrc[d * 16 : (d + 1) * 16] = x_ref[code % 64] * mine
    parts = []
    for dr in range(1, 16):
        there = lax.rem(r + dr, 16)
        h = pltpu.make_async_remote_copy(
            src_ref=dsrc.at[pl.ds(there * slots, slots)], dst_ref=rr.at[dr],
            send_sem=sc.at[dr], recv_sem=qc.at[dr], device_id=across(dr), device_id_type=MESH,
        )
        h.start()
        parts.append(h)
    total = dsrc[pl.ds(pl.multiple_of(r * slots, 8), slots)]
    for dr, h in zip(range(1, 16), parts):
        h.wait_recv()
        total = total + rr[dr]
    piece[...] = total.reshape(piece.shape)

    outs = []
    for dy in (2, 1, 3):
        h = pltpu.make_async_remote_copy(
            src_ref=piece, dst_ref=d_ref.at[z, x, :, c],
            send_sem=sd.at[dy], recv_sem=qd.at[c], device_id=to_half(dy), device_id_type=MESH,
        )
        h.start()
        outs.append(h)
    near = pltpu.make_async_remote_copy(
        src_ref=piece, dst_ref=d_ref.at[z, x, :, c],
        send_sem=sd.at[0], recv_sem=qd.at[c], device_id=other, device_id_type=MESH,
    )

    @pl.when(inside)
    def _():
        d_ref[z, x, :, c] = piece[...]

    @pl.when(jnp.logical_not(inside))
    def _():
        near.start()

    for q in range(4):
        source = 4 * k + q

        @pl.when(source != c)
        def _():
            pltpu.make_async_remote_copy(
                src_ref=piece, dst_ref=d_ref.at[z, x, :, source],
                send_sem=sd.at[0], recv_sem=qd.at[source], device_id=other, device_id_type=MESH,
            ).wait_recv()

    def move(ref, i, device):
        h = pltpu.make_async_remote_copy(
            src_ref=ref, dst_ref=ref, send_sem=se.at[i], recv_sem=qe.at[i],
            device_id=device, device_id_type=MESH,
        )
        h.start()
        return h

    def twin(ref, i):
        h = pltpu.make_async_remote_copy(
            src_ref=ref, dst_ref=ref, send_sem=sf.at[i], recv_sem=qf.at[i],
            device_id=other, device_id_type=MESH,
        )
        h.start()
        twins.append(h)

    part_x, part_z = pl.ds(4 * k, 2), pl.ds(4 * k + 2, 2)
    near_x, near_z, far_x, far_z, twins = [], [], [], [], []
    for d in (2, 1, 3):
        near_x.append(move(d_ref.at[z, x, :, part_x], d, along_x(d)))
        near_z.append(move(d_ref.at[z, x, :, part_z], 4 + d, along_z(d)))
    for h in near_x:
        h.wait_recv()
    for d in (2, 1, 3):
        far_x.append((d, move(d_ref.at[z, :, :, part_x], 8 + d, along_z(d))))
    for h in near_z:
        h.wait_recv()
    for d in (2, 1, 3):
        far_z.append((d, move(d_ref.at[:, x, :, part_z], 12 + d, along_x(d))))
    twin(d_ref.at[z, :, :, part_x], 0)
    twin(d_ref.at[:, x, :, part_z], 4)
    for i in (1, 2, 0):
        d, h = far_x[i]
        h.wait_recv()
        twin(d_ref.at[lax.rem(z + 4 - d, 4), :, :, part_x], d)
        d, h = far_z[i]
        h.wait_recv()
        twin(d_ref.at[:, lax.rem(x + 4 - d, 4), :, part_z], 4 + d)
    wholes = near_x + near_z + [h for _, h in far_x + far_z]
    for t in twins:
        t.wait()
    for _, _, h in halves:
        h.wait_send()
    for _, q in quarters:
        q.wait_send()
    for h in parts + wholes + outs:
        h.wait_send()

    @pl.when(jnp.logical_not(inside))
    def _():
        near.wait_send()


def gather(meta, given):
    slots = given.shape[1]
    vmem = pl.BlockSpec(memory_space=pltpu.VMEM)
    dma = pltpu.SemaphoreType.DMA
    return pl.pallas_call(
        gather_kernel,
        out_shape=(
            jax.ShapeDtypeStruct((slots, 16, 128), F32),
            jax.ShapeDtypeStruct((4, 4, slots // 16, 8, 16, 128), F32),
        ),
        in_specs=[pl.BlockSpec(memory_space=pltpu.SMEM), vmem],
        out_specs=(vmem, vmem),
        scratch_shapes=[
            pltpu.VMEM((4, slots, 16, 128), F32),
            pltpu.VMEM((4, slots, 16, 128), F32),
            pltpu.VMEM((4, slots, 16, 128), F32),
            pltpu.VMEM((slots * 16, 128), F32),
            pltpu.VMEM((16, slots, 128), F32),
            pltpu.VMEM((slots // 16, 16, 128), F32),
            dma((4,)), dma((4,)), dma((4,)), dma((4,)),
            dma((16,)), dma((16,)), dma((4,)), dma((8,)),
            dma((16,)), dma((16,)), dma((8,)), dma((8,)),
        ],
        compiler_params=pltpu.CompilerParams(
            collective_id=slots, has_side_effects=True, vmem_limit_bytes=48 << 20
        ),
        name="gather",
    )(meta, given.reshape(4, 2, slots, 16, 128))


def lane(x, i):
    return jnp.take_along_axis(x, jnp.full(x.shape, i, jnp.int32), axis=1)


def pivots(us, vs, first):
    e = {}
    for i in range(8):
        for k in range(i + 1):
            e[i, k] = lane(us[i], first + k)
    f = {}
    for k in range(8):
        f[k, k] = lax.rsqrt(e[k, k])
        for i in range(k + 1, 8):
            f[i, k] = e[i, k] * f[k, k]
        for i in range(k + 1, 8):
            for m in range(k + 1, i + 1):
                e[i, m] = e[i, m] - f[i, k] * f[m, k]
    outs, outv = [], []
    for k in range(8):
        u, v = us[k], vs[k]
        for m in range(k):
            u = u - f[k, m] * outs[m]
            v = v - f[k, m] * outv[m]
        outs.append(u * f[k, k])
        outv.append(v * f[k, k])
    return outs, outv


def split(x):
    high = x.astype(BF16)
    x = x - high.astype(F32)
    middle = x.astype(BF16)
    return high, middle, (x - middle.astype(F32)).astype(BF16)


def batched_inverse(st, ht, ub, vb, count):
    lanes = lax.broadcasted_iota(jnp.int32, (16, 128), 1)

    @pl.loop(0, 8)
    def _(c):
        base = c * 16
        us = [st[pl.ds(base + k, 8, stride=128)] for k in range(16)]
        vs = [ht[pl.ds(base + k, 8, stride=128)] for k in range(16)]
        us[:8], vs[:8] = pivots(us[:8], vs[:8], base)
        for m in range(8, 16):
            for k in range(8):
                w = lane(us[k], base + m)
                us[m] = us[m] - w * us[k]
                vs[m] = vs[m] - w * vs[k]
        us[8:], vs[8:] = pivots(us[8:], vs[8:], base + 8)
        for k in range(16):
            ht[pl.ds(base + k, 8, stride=128)] = vs[k]
            ub[pl.ds(k, 8, stride=16)] = us[k]
            vb[pl.ds(k, 8, stride=16)] = vs[k]

        @pl.when(c < 7)
        def _():
            @pl.loop(0, (count + GROUP - 1) // GROUP)
            def _(q):
                for t in range(GROUP):
                    b = q * GROUP + t
                    here = pl.ds(pl.multiple_of(b * 16, 16), 16)
                    u = ub[here]
                    x, y, z = split(jnp.where(lanes >= base + 16, u, 0.0))
                    left = jnp.concatenate([x, x, y, y, x, z], axis=0)
                    x, y, z = split(jnp.concatenate([u, vb[here]], axis=1))
                    right = jnp.concatenate([x, y, x, y, z, x], axis=0)
                    change = lax.dot_general(
                        left, right, (((0,), (0,)), ((), ())), preferred_element_type=F32
                    )
                    rows = pl.ds(pl.multiple_of(b * 128, 128), 128)
                    st[rows] -= change[:, :128]
                    ht[rows] -= change[:, 128:]


def factor_kernel(meta, x_ref, d_ref, out_ref, st, ht, ub, vb, g, f, s, w, ld, lf):
    def same(i, j):
        return meta[SLOTD + i, j] >= 0

    def held(value, i, j):
        return jnp.where(i // SUPER < j // SUPER, value.astype(BF16).astype(F32), value)

    def block(i, j):
        return d_ref[meta[SLOTD + i, j]]

    st[...] = jnp.zeros_like(st)
    unit = lax.broadcasted_iota(jnp.int32, (128, 128), 0) == lax.broadcasted_iota(
        jnp.int32, (128, 128), 1
    )

    @pl.loop(0, meta[SIZES, 1])
    def _(level):
        for b in range(8):
            ht[b * 128 : (b + 1) * 128] = unit.astype(F32)

        @pl.loop(0, PICKS)
        def _(j):
            @pl.when(meta[LEVEL, j] == level)
            def _():
                s[...] = block(j, j)

                @pl.loop(0, j)
                def _(i):
                    @pl.when(same(j, i))
                    def _():
                        w[...] = block(j, i)

                        @pl.loop(0, i)
                        def _(m):
                            @pl.when(same(j, m))
                            def _():
                                w[...] -= dot_nt(
                                    held(f[j * PICKS + m], m, i), held(f[i * PICKS + m], m, i)
                                )

                        done = dot_nt(w[...], g[i])
                        f[j * PICKS + i] = done
                        done = held(done, i, j)
                        s[...] -= dot_nt(done, done)

                st[pl.ds(pl.multiple_of(meta[SPOT, j] * 128, 128), 128)] = s[...]

        batched_inverse(st, ht, ub, vb, meta[COUNT, level])

        @pl.loop(0, PICKS)
        def _(j):
            @pl.when(meta[LEVEL, j] == level)
            def _():
                g[j] = ht[pl.ds(pl.multiple_of(meta[SPOT, j] * 128, 128), 128)]

    my_row = lax.axis_index("row")
    last = out_ref.shape[0] - 1
    for a in range(8):
        for j in range(PICKS):
            slot = meta[j, a * 16 + my_row]
            ld[j, a * 16 : (a + 1) * 16] = jnp.where(slot >= 0, x_ref[jnp.maximum(slot, 0)], 0.0)

    for j in range(PICKS):
        lf[j] = dot_nt(ld[j], g[j])

    @pl.loop(1, PICKS)
    def _(j):
        @pl.when(meta[LEVEL, j] > 0)
        def _():
            @pl.loop(0, j)
            def _(i):
                @pl.when(same(j, i))
                def _():
                    ld[j] -= dot_nt(held(lf[i], i, j), held(f[j * PICKS + i], i, j))

            lf[j] = dot_nt(ld[j], g[j])

    for a in range(8):
        elim = meta[ELIM, a * 16 + my_row]
        for j in range(PICKS):
            slot = meta[j, a * 16 + my_row]
            alive = (elim < 0) | (elim >= (j // SUPER + 1) * SUPER)
            rows = jnp.where(alive, lf[j, a * 16 : (a + 1) * 16], 0.0)
            out_ref[jnp.where(slot >= 0, slot, last)] = rows.astype(BF16)


def factor(meta, x, d):
    slots = x.shape[0]
    vmem = pl.BlockSpec(memory_space=pltpu.VMEM)
    return pl.pallas_call(
        factor_kernel,
        out_shape=jax.ShapeDtypeStruct((slots + 1, 16, 128), BF16),
        in_specs=[pl.BlockSpec(memory_space=pltpu.SMEM), vmem, vmem],
        out_specs=vmem,
        scratch_shapes=[
            pltpu.VMEM((1024, 128), F32),
            pltpu.VMEM((1024, 128), F32),
            pltpu.VMEM((128, 128), F32),
            pltpu.VMEM((128, 128), F32),
            pltpu.VMEM((8, 128, 128), F32),
            pltpu.VMEM((64, 128, 128), F32),
            pltpu.VMEM((128, 128), F32),
            pltpu.VMEM((128, 128), F32),
            pltpu.VMEM((8, 128, 128), F32),
            pltpu.VMEM((8, 128, 128), F32),
        ],
        compiler_params=pltpu.CompilerParams(vmem_limit_bytes=48 << 20),
        name="factor",
    )(meta, x, d.reshape(slots, 128, 128))


def share_kernel(l_ref, row_ref, col_ref, se, qe, sf, qf, sg, qg, sx, qx, sz, qz):
    slots = l_ref.shape[0] - 1
    n = slots // 16
    r, c, y, k = place()
    z, x = r // 4, lax.rem(r, 4)
    other = {"row": r, "col": y * 2 + 1 - k}
    goal = lax.rem(r, 8)
    high = r // 8

    def along(dy):
        return {"row": r, "col": lax.rem(y + dy, 4) * 2 + k}

    def along_x(d):
        return {"row": z * 4 + lax.rem(x + d, 4), "col": c}

    def along_z(d):
        return {"row": lax.rem(z + d, 4) * 4 + x, "col": c}

    def greet(device):
        pl.semaphore_signal(barrier, inc=1, device_id=device, device_id_type=MESH)

    barrier = pltpu.get_barrier_semaphore()
    greet(other)
    for d in (1, 2, 3):
        greet(along(d))
        greet(along_x(d))
        greet(along_z(d))
    for q in range(16):
        source = c + (q // 8) * 8
        far = jnp.logical_not((source == r) & (q % 8 == c))

        @pl.when(far)
        def _():
            greet({"row": source, "col": q % 8})

    pl.semaphore_wait(barrier, 25 + jnp.where(goal == c, 0, 1))

    def send(d):
        m = lax.rem(r + d, 16)
        return pltpu.make_async_remote_copy(
            src_ref=l_ref.at[pl.ds(m * n, n)],
            dst_ref=col_ref.at[high, m // 4, lax.rem(m, 4), :, c],
            send_sem=sg.at[d], recv_sem=qg.at[high * 8 + c],
            device_id={"row": m, "col": goal}, device_id_type=MESH,
        )

    for d in range(1, 16):
        send(d).start()

    @pl.when(goal == c)
    def _():
        col_ref[high, z, x, :, c] = l_ref[pl.ds(r * n, n)]

    @pl.when(goal != c)
    def _():
        send(0).start()

    row_ref[y, k] = l_ref[:slots]
    outs = []
    for d in (2, 1, 3):
        h = pltpu.make_async_remote_copy(
            src_ref=row_ref.at[y, k], dst_ref=row_ref.at[y, k],
            send_sem=se.at[d], recv_sem=qe.at[d], device_id=along(d), device_id_type=MESH,
        )
        h.start()
        outs.append((d, h))

    def move(ref, s, q, device):
        h = pltpu.make_async_remote_copy(
            src_ref=ref, dst_ref=ref, send_sem=s, recv_sem=q, device_id=device, device_id_type=MESH
        )
        h.start()
        return h

    near = []
    for half in range(2):
        for q in range(half * 8, half * 8 + 8):
            far = jnp.logical_not((c + half * 8 == r) & (q % 8 == c))

            @pl.when(far)
            def _():
                pltpu.make_async_remote_copy(
                    src_ref=l_ref.at[pl.ds(0, n)], dst_ref=col_ref.at[half, z, x, :, q % 8],
                    send_sem=sg.at[0], recv_sem=qg.at[q], device_id=other, device_id_type=MESH,
                ).wait_recv()

        for d in (2, 1, 3):
            if half == 0:
                near.append(move(col_ref.at[0, z, x], sx.at[d], qx.at[d], along_x(d)))
            else:
                near.append(move(col_ref.at[1, z, x], sz.at[d], qz.at[d], along_z(d)))

    twins = []
    for d in (0, 1, 3, 2):
        come = lax.rem(y + 4 - d, 4)
        for e, h in outs:
            if e == d:
                h.wait_recv()
        twins.append(move(row_ref.at[come, k], sf.at[d], qf.at[d], other))

    for h in near:
        h.wait_recv()
    last = []
    for d in (2, 1, 3):
        last.append(move(col_ref.at[0, z], sx.at[3 + d], qx.at[3 + d], along_z(d)))
        last.append(move(col_ref.at[1, :, x], sz.at[3 + d], qz.at[3 + d], along_x(d)))
    for h in twins + last:
        h.wait()
    for h in near + [h for _, h in outs]:
        h.wait_send()
    for d in range(1, 16):
        send(d).wait_send()

    @pl.when(goal != c)
    def _():
        send(0).wait_send()


def share(l):
    slots = l.shape[0] - 1
    vmem = pl.BlockSpec(memory_space=pltpu.VMEM)
    dma = pltpu.SemaphoreType.DMA
    return pl.pallas_call(
        share_kernel,
        out_shape=(
            jax.ShapeDtypeStruct((4, 2, slots, 16, 128), BF16),
            jax.ShapeDtypeStruct((2, 4, 4, slots // 16, 8, 16, 128), BF16),
        ),
        in_specs=[vmem],
        out_specs=(vmem, vmem),
        scratch_shapes=[
            dma((4,)), dma((4,)), dma((4,)), dma((4,)), dma((16,)), dma((16,)),
            dma((7,)), dma((7,)), dma((7,)), dma((7,)),
        ],
        compiler_params=pltpu.CompilerParams(
            collective_id=slots + 1, has_side_effects=True, vmem_limit_bytes=48 << 20
        ),
        name="share",
    )(l)


def update_kernel(meta, a_ref, row_ref, col_ref, panel_ref, out_ref, held, sems):
    a = pl.program_id(0)
    my_col = lax.axis_index("col")
    my_row = lax.axis_index("row")

    def fetch(a, n):
        b = meta[LIST + n, a * 16 + my_row]
        place = lax.rem(a, AHEAD)
        return pltpu.make_async_copy(a_ref.at[a, b], held.at[place, n], sems.at[place, n])

    def ask(a):
        @pl.loop(0, meta[HITS, a * 16 + my_row])
        def _(n):
            fetch(a, n).start()

    @pl.when(a == 0)
    def _():
        for t in range(AHEAD - 1):
            ask(t)

    @pl.when(a < 9 - AHEAD)
    def _():
        ask(a + AHEAD - 1)

    g = a * 16 + my_row
    panel_ref[...] = jnp.zeros_like(panel_ref)
    out_ref[...] = jnp.zeros_like(out_ref)
    number = meta[NUMBER, g]

    def left(slot):
        return row_ref[:, slot].reshape(128, 128)

    def product(x, y):
        return lax.dot_general(x, y, NT, preferred_element_type=F32)

    @pl.when(number > 0)
    def _():
        for j in range(PICKS):
            @pl.when(meta[j, g] >= 0)
            def _():
                lanes = slice((j % SUPER) * 128, (j % SUPER + 1) * 128)
                panel_ref[j // SUPER, 0, :, lanes] = left(meta[j, g])

    @pl.loop(0, meta[HITS, g])
    def _(n):
        b = meta[LIST + n, g]
        h = b * 8 + my_col
        half = lax.rem(b, 2)
        fetch(a, n).wait()
        value = held.at[lax.rem(a, AHEAD), n]

        @pl.when(number == 0)
        def _():
            out_ref[0, b] = value[...]

        @pl.when(number == 1)
        def _():
            out_ref[0, b] = value[...] - product(left(meta[ONE, g]), col_ref[half, meta[ONE, h]])

        @pl.when(number >= 2)
        def _():
            out_ref[0, b] = value[...] - product(
                jnp.concatenate([left(meta[ONE, g]), left(meta[TWO, g])], axis=1),
                jnp.concatenate([col_ref[half, meta[ONE, h]], col_ref[half, meta[TWO, h]]], axis=1),
            )

        @pl.when(number >= 3)
        def _():
            @pl.loop(0, PICKS)
            def _(j):
                @pl.when((meta[j, g] >= 0) & (meta[LEVEL, j] >= 2))
                def _():
                    out_ref[0, b] -= product(left(meta[j, g]), col_ref[half, meta[j, h]])


def update(meta, blocks, rows, cols):
    slots = rows.shape[2]
    whole = lambda n: (lambda a, m: (0,) * n)
    return pl.pallas_call(
        update_kernel,
        grid_spec=pltpu.PrefetchScalarGridSpec(
            num_scalar_prefetch=1,
            grid=(8,),
            in_specs=[
                pl.BlockSpec(memory_space=pl.ANY),
                pl.BlockSpec((8, slots, 16, 128), whole(4)),
                pl.BlockSpec((2, slots, 128, 128), whole(4)),
            ],
            out_specs=[
                pl.BlockSpec((2, 1, 128, 512), lambda a, m: (0, a, 0, 0)),
                pl.BlockSpec((1, 16, 128, 128), lambda a, m: (a, 0, 0, 0)),
            ],
            scratch_shapes=[
                pltpu.VMEM((AHEAD, 16, 128, 128), F32),
                pltpu.SemaphoreType.DMA((AHEAD, 16)),
            ],
        ),
        out_shape=(
            jax.ShapeDtypeStruct((2, 8, 128, 512), BF16),
            jax.ShapeDtypeStruct((8, 16, 128, 128), F32),
        ),
        compiler_params=pltpu.CompilerParams(vmem_limit_bytes=48 << 20),
        name="update",
    )(meta, blocks, rows.reshape(8, slots, 16, 128), cols.reshape(2, slots, 128, 128))


def ranks(marks, before):
    total = jnp.sum(marks, axis=0, keepdims=True)
    run = jnp.dot(jnp.broadcast_to(total, (8, 128)), before, preferred_element_type=F32)[:1]
    rows = []
    for j in range(8):
        rows.append(jnp.where(marks[j : j + 1] > 0, run, -1.0))
        run = run + marks[j : j + 1]
    return jnp.concatenate(rows, axis=0), jnp.max(run, axis=1, keepdims=True)


def tables_kernel(order, pattern_ref, meta_ref):
    lanes = lax.broadcasted_iota(jnp.int32, (8, 128), 1)
    rows = lax.broadcasted_iota(jnp.int32, (8, 128), 0)
    lane = lanes[:1]
    g = lax.broadcasted_iota(jnp.int32, (128, 128), 0)
    h = lax.broadcasted_iota(jnp.int32, (128, 128), 1)
    onehot = jnp.zeros((8, 128), F32)
    target = jnp.zeros((1, 128), jnp.int32)
    for j in range(PICKS):
        onehot = jnp.where((rows == j) & (lanes == order[j]), 1.0, onehot)
        target = jnp.where(lane == j, order[j], target)
    linked = pattern_ref[...].astype(F32)
    pad = lambda x: jnp.concatenate([x, jnp.zeros((120, 128), F32)], axis=0)
    small = lambda a, b: lax.dot_general(a, b, NT, preferred_element_type=F32)
    member = jnp.dot(onehot, linked, preferred_element_type=F32)
    slot, full = ranks(member, (((g & 15) == (h & 15)) & (g < h)).astype(F32))
    among = small(onehot, pad(member))
    lower = jnp.where(lanes <= rows, among, 0.0)
    upper = jnp.where(rows <= lanes, among, 0.0)
    slotd, fulld = ranks(lower, (g < h).astype(F32))
    home = jnp.sum(onehot * (lanes & 15).astype(F32), axis=1, keepdims=True)
    code = home * 64.0 + small(onehot, pad(slot))
    source = jnp.zeros((8, 128), F32)
    for j in range(PICKS):
        source = source + jnp.where(slotd[:, j : j + 1] == lanes.astype(F32), code[:, j : j + 1], 0.0)
    source = jnp.sum(source, axis=0, keepdims=True)
    source = jnp.where(lane.astype(F32) < fulld, source, 1024.0)
    down = jnp.sum(lower, axis=1, keepdims=True) - 1.0
    level = jnp.sum(upper, axis=0, keepdims=True) - 1.0
    spot = jnp.sum(jnp.where((down == level) & (rows < lanes), 1.0, 0.0), axis=0, keepdims=True)
    count = jnp.sum(jnp.where(down == lanes.astype(F32), 1.0, 0.0), axis=0, keepdims=True)
    depth = jnp.max(down, axis=0, keepdims=True) + 1.0
    sizes = jnp.where(lane == 0, jnp.maximum(full, fulld), depth)
    elim = jnp.sum(onehot * (rows + 1).astype(F32), axis=0, keepdims=True) - 1.0
    label = jnp.min(jnp.where(linked > 0, g.astype(F32), 999.0), axis=0, keepdims=True)

    def put(row, value):
        meta_ref[row : row + value.shape[0]] = value.astype(jnp.int32)

    put(0, slot)
    put(LABEL, label)
    put(ELIM, elim)
    put(TARGET, target)
    put(LEVEL, level)
    put(SPOT, spot)
    put(COUNT, count)
    put(SOURCE, source)
    put(SIZES, sizes)
    put(SLOTD, slotd)
    rows16 = lax.broadcasted_iota(jnp.int32, (16, 128), 0)
    lanes16 = lax.broadcasted_iota(jnp.int32, (16, 128), 1)
    mine = (lanes16 == rows16 * 8 + lax.axis_index("col")).astype(F32)
    held = jnp.dot(mine, linked, preferred_element_type=F32)
    run = jnp.zeros((1, 128), F32)
    listed = jnp.zeros((16, 128), F32)
    for b in range(16):
        here = held[b : b + 1]
        listed = jnp.where((here > 0) & (run == rows16.astype(F32)), float(b), listed)
        run = run + here
    put(HITS, run)
    put(LIST, listed)
    put(NUMBER, jnp.sum(member, axis=0, keepdims=True))
    for row, order_in in ((ONE, 0.0), (TWO, 1.0)):
        taken = jnp.where((member > 0) & (down == order_in), slot + 1.0, 0.0)
        put(row, jnp.sum(taken, axis=0, keepdims=True) - 1.0)


def tables(pattern, order):
    vmem = pl.BlockSpec(memory_space=pltpu.VMEM)
    return pl.pallas_call(
        tables_kernel,
        out_shape=jax.ShapeDtypeStruct((48, 128), jnp.int32),
        in_specs=[pl.BlockSpec(memory_space=pltpu.SMEM), vmem],
        out_specs=vmem,
        name="tables",
    )(order, pattern)


def compact(slots, meta, blocks):
    given = pick(slots, meta, blocks.reshape(8, 16, 8, 16, 128))
    x, d = gather(meta, given)
    l = factor(meta, x, d)
    rows, cols = share(l)
    return update(meta, blocks, rows, cols)


def shards(matrix_blocks, pattern, order):
    local = matrix_blocks[:, 0, :, 0]
    meta = tables(pattern, order)
    tier = sum((meta[SIZES, 0] > slots).astype(jnp.int32) for slots in TIERS[:-1])
    ways = [functools.partial(compact, slots, meta, local) for slots in TIERS]
    panels, trailing = lax.switch(tier, ways)
    return panels[:, :, None], trailing[:, None, :, None]


def solution(mesh):
    in_specs = (P(None, "row", None, "col", None, None), P(), P())
    out_specs = (P(None, None, "row", None, None), P(None, "row", None, "col", None, None))
    return jax.shard_map(shards, mesh=mesh, in_specs=in_specs, out_specs=out_specs, check_vma=False)
```

```python
import functools

import jax
import jax.numpy as jnp
from jax import lax
from jax.experimental import pallas as pl
from jax.experimental.pallas import tpu as pltpu
from jax.sharding import PartitionSpec as P

SUPER = 4
WAVE = 4
PICKS = 8
TIERS = (16, 32, 64)
MESH = pl.DeviceIdType.MESH
HIGH = lax.Precision.HIGHEST
F32 = jnp.float32
BF16 = jnp.bfloat16
NT = (((1,), (1,)), ((), ()))

LABEL = 8
ELIM = 9
TARGET = 10
LEVEL = 11
SPOT = 12
SOURCE = 14
SIZES = 15
NUMBER = 24
ONE = 25
TWO = 26
HITS = 27
LIST = 32
SLOTD = 16


def dot_nt(a, b):
    return lax.dot_general(a, b, NT, precision=HIGH, preferred_element_type=F32)


def pick_kernel(meta, a_ref, out_ref, sems):
    my_row = lax.axis_index("row")
    my_col = lax.axis_index("col")
    out_ref[...] = jnp.zeros_like(out_ref)

    def each(act):
        @pl.loop(0, PICKS)
        def _(j):
            target = meta[TARGET, j]

            @pl.when(target % 8 == my_col)
            def _():
                for a in range(8):
                    slot = meta[j, a * 16 + my_row]

                    @pl.when(slot >= 0)
                    def _():
                        act(
                            pltpu.make_async_copy(
                                a_ref.at[a, target // 8], out_ref.at[:, slot], sems.at[slot]
                            )
                        )

    each(lambda copy: copy.start())
    each(lambda copy: copy.wait())


def pick(slots, meta, blocks):
    return pl.pallas_call(
        pick_kernel,
        out_shape=jax.ShapeDtypeStruct((8, slots, 16, 128), F32),
        in_specs=[pl.BlockSpec(memory_space=pltpu.SMEM), pl.BlockSpec(memory_space=pl.ANY)],
        out_specs=pl.BlockSpec(memory_space=pltpu.VMEM),
        scratch_shapes=[pltpu.SemaphoreType.DMA((slots,))],
        compiler_params=pltpu.CompilerParams(vmem_limit_bytes=24 << 20),
        name="pick",
    )(meta, blocks)


def place():
    r = lax.axis_index("row")
    c = lax.axis_index("col")
    return r, c, c // 2, c % 2


def gather_kernel(
    meta, give_ref, x_ref, d_ref, ra, acc, rb, dsrc, rr, piece,
    sa, qa, sb, qb, sc, qc, sd, qd, se, qe, sf, qf,
):
    slots = x_ref.shape[0]
    r, c, y, k = place()
    other = {"row": r, "col": y * 2 + 1 - k}

    def along(dy):
        return {"row": r, "col": lax.rem(y + dy, 4) * 2 + k}

    def across(dr):
        return {"row": lax.rem(r + dr, 16), "col": c}

    z, x = r // 4, lax.rem(r, 4)

    def along_x(d):
        return {"row": z * 4 + lax.rem(x + d, 4), "col": c}

    def along_z(d):
        return {"row": lax.rem(z + d, 4) * 4 + x, "col": c}

    inside = y // 2 == k

    def to_half(dy):
        return {"row": r, "col": lax.rem(y + dy, 4) * 2 + y // 2}

    barrier = pltpu.get_barrier_semaphore()
    pl.semaphore_signal(barrier, inc=1, device_id=other, device_id_type=MESH)
    for dy in (1, 2, 3):
        pl.semaphore_signal(barrier, inc=1, device_id=along(dy), device_id_type=MESH)
    for dr in range(1, 16):
        pl.semaphore_signal(barrier, inc=1, device_id=across(dr), device_id_type=MESH)
    for q in range(4):
        @pl.when(4 * k + q != c)
        def _():
            pl.semaphore_signal(
                barrier, inc=1, device_id={"row": r, "col": 4 * k + q}, device_id_type=MESH
            )

    pl.semaphore_wait(barrier, 22 + jnp.where(inside, 0, 1))

    halves = []
    for dy in (2, 1, 3, 0):
        there = lax.rem(y + dy, 4)
        h = pltpu.make_async_remote_copy(
            src_ref=give_ref.at[there, 1 - k], dst_ref=ra.at[dy],
            send_sem=sa.at[dy], recv_sem=qa.at[dy], device_id=other, device_id_type=MESH,
        )
        h.start()
        halves.append((dy, there, h))
    quarters = []
    for dy, there, h in halves:
        h.wait_recv()
        if dy:
            acc[dy] = give_ref[there, k] + ra[dy]
            q = pltpu.make_async_remote_copy(
                src_ref=acc.at[dy], dst_ref=rb.at[dy],
                send_sem=sb.at[dy], recv_sem=qb.at[dy], device_id=along(dy), device_id_type=MESH,
            )
            q.start()
            quarters.append((dy, q))
        else:
            total = give_ref[there, k] + ra[dy]
    for dy, q in quarters:
        q.wait_recv()
        total = total + rb[dy]
    x_ref[...] = total

    for d in range(slots):
        code = meta[SOURCE, d]
        mine = (code // 64 == r).astype(F32)
        dsrc[d * 16 : (d + 1) * 16] = x_ref[code % 64] * mine
    parts = []
    for dr in range(1, 16):
        there = lax.rem(r + dr, 16)
        h = pltpu.make_async_remote_copy(
            src_ref=dsrc.at[pl.ds(there * slots, slots)], dst_ref=rr.at[dr],
            send_sem=sc.at[dr], recv_sem=qc.at[dr], device_id=across(dr), device_id_type=MESH,
        )
        h.start()
        parts.append(h)
    total = dsrc[pl.ds(pl.multiple_of(r * slots, 8), slots)]
    for dr, h in zip(range(1, 16), parts):
        h.wait_recv()
        total = total + rr[dr]
    piece[...] = total.reshape(piece.shape)

    outs = []
    for dy in (2, 1, 3):
        h = pltpu.make_async_remote_copy(
            src_ref=piece, dst_ref=d_ref.at[z, x, :, c],
            send_sem=sd.at[dy], recv_sem=qd.at[c], device_id=to_half(dy), device_id_type=MESH,
        )
        h.start()
        outs.append(h)
    near = pltpu.make_async_remote_copy(
        src_ref=piece, dst_ref=d_ref.at[z, x, :, c],
        send_sem=sd.at[0], recv_sem=qd.at[c], device_id=other, device_id_type=MESH,
    )

    @pl.when(inside)
    def _():
        d_ref[z, x, :, c] = piece[...]

    @pl.when(jnp.logical_not(inside))
    def _():
        near.start()

    for q in range(4):
        source = 4 * k + q

        @pl.when(source != c)
        def _():
            pltpu.make_async_remote_copy(
                src_ref=piece, dst_ref=d_ref.at[z, x, :, source],
                send_sem=sd.at[0], recv_sem=qd.at[source], device_id=other, device_id_type=MESH,
            ).wait_recv()

    def move(ref, i, device):
        h = pltpu.make_async_remote_copy(
            src_ref=ref, dst_ref=ref, send_sem=se.at[i], recv_sem=qe.at[i],
            device_id=device, device_id_type=MESH,
        )
        h.start()
        return h

    def twin(ref, i):
        h = pltpu.make_async_remote_copy(
            src_ref=ref, dst_ref=ref, send_sem=sf.at[i], recv_sem=qf.at[i],
            device_id=other, device_id_type=MESH,
        )
        h.start()
        twins.append(h)

    part_x, part_z = pl.ds(4 * k, 2), pl.ds(4 * k + 2, 2)
    near_x, near_z, far_x, far_z, twins = [], [], [], [], []
    for d in (2, 1, 3):
        near_x.append(move(d_ref.at[z, x, :, part_x], d, along_x(d)))
        near_z.append(move(d_ref.at[z, x, :, part_z], 4 + d, along_z(d)))
    for h in near_x:
        h.wait_recv()
    for d in (2, 1, 3):
        far_x.append((d, move(d_ref.at[z, :, :, part_x], 8 + d, along_z(d))))
    for h in near_z:
        h.wait_recv()
    for d in (2, 1, 3):
        far_z.append((d, move(d_ref.at[:, x, :, part_z], 12 + d, along_x(d))))
    twin(d_ref.at[z, :, :, part_x], 0)
    twin(d_ref.at[:, x, :, part_z], 4)
    for i in (1, 2, 0):
        d, h = far_x[i]
        h.wait_recv()
        twin(d_ref.at[lax.rem(z + 4 - d, 4), :, :, part_x], d)
        d, h = far_z[i]
        h.wait_recv()
        twin(d_ref.at[:, lax.rem(x + 4 - d, 4), :, part_z], 4 + d)
    wholes = near_x + near_z + [h for _, h in far_x + far_z]
    for t in twins:
        t.wait()
    for _, _, h in halves:
        h.wait_send()
    for _, q in quarters:
        q.wait_send()
    for h in parts + wholes + outs:
        h.wait_send()

    @pl.when(jnp.logical_not(inside))
    def _():
        near.wait_send()


def gather(meta, given):
    slots = given.shape[1]
    vmem = pl.BlockSpec(memory_space=pltpu.VMEM)
    dma = pltpu.SemaphoreType.DMA
    return pl.pallas_call(
        gather_kernel,
        out_shape=(
            jax.ShapeDtypeStruct((slots, 16, 128), F32),
            jax.ShapeDtypeStruct((4, 4, slots // 16, 8, 16, 128), F32),
        ),
        in_specs=[pl.BlockSpec(memory_space=pltpu.SMEM), vmem],
        out_specs=(vmem, vmem),
        scratch_shapes=[
            pltpu.VMEM((4, slots, 16, 128), F32),
            pltpu.VMEM((4, slots, 16, 128), F32),
            pltpu.VMEM((4, slots, 16, 128), F32),
            pltpu.VMEM((slots * 16, 128), F32),
            pltpu.VMEM((16, slots, 128), F32),
            pltpu.VMEM((slots // 16, 16, 128), F32),
            dma((4,)), dma((4,)), dma((4,)), dma((4,)),
            dma((16,)), dma((16,)), dma((4,)), dma((8,)),
            dma((16,)), dma((16,)), dma((8,)), dma((8,)),
        ],
        compiler_params=pltpu.CompilerParams(
            collective_id=slots, has_side_effects=True, vmem_limit_bytes=48 << 20
        ),
        name="gather",
    )(meta, given.reshape(4, 2, slots, 16, 128))


def lane(x, i):
    if isinstance(i, int):
        return jnp.broadcast_to(x[:, i : i + 1], x.shape)
    return jnp.take_along_axis(x, jnp.full(x.shape, i, jnp.int32), axis=1)


def pivots(us, vs, first):
    e = {}
    for i in range(8):
        for k in range(i + 1):
            e[i, k] = lane(us[i], first + k)
    f = {}
    for k in range(8):
        f[k, k] = lax.rsqrt(e[k, k])
        for i in range(k + 1, 8):
            f[i, k] = e[i, k] * f[k, k]
        for i in range(k + 1, 8):
            for m in range(k + 1, i + 1):
                e[i, m] = e[i, m] - f[i, k] * f[m, k]
    outs, outv = [], []
    for k in range(8):
        u, v = us[k], vs[k]
        for m in range(k):
            u = u - f[k, m] * outs[m]
            v = v - f[k, m] * outv[m]
        outs.append(u * f[k, k])
        outv.append(v * f[k, k])
    return outs, outv


def split(x):
    high = x.astype(BF16)
    x = x - high.astype(F32)
    middle = x.astype(BF16)
    return high, middle, (x - middle.astype(F32)).astype(BF16)


def batched_inverse(st, ub, vb):
    lanes = lax.broadcasted_iota(jnp.int32, (8, 128), 1)
    for c in range(8):
        base, end = c * 16, c * 16 + 16
        us = [st[pl.ds(base + k, 8, stride=128)] for k in range(16)]
        vs = [
            jnp.where(lanes < base, us[k], (lanes == base + k).astype(F32)) for k in range(16)
        ]
        us[:8], vs[:8] = pivots(us[:8], vs[:8], base)
        for m in range(8, 16):
            for k in range(8):
                w = lane(us[k], base + m)
                us[m] = us[m] - w * us[k]
                vs[m] = vs[m] - w * vs[k]
        us[8:], vs[8:] = pivots(us[8:], vs[8:], base + 8)
        for k in range(16):
            st[pl.ds(base + k, 8, stride=128)] = vs[k]
            ub[pl.ds(k, 8, stride=16)] = jnp.where(lanes < end, 0.0, us[k])
            vb[pl.ds(k, 8, stride=16)] = jnp.where(lanes < end, vs[k], us[k])
        if c == 7:
            continue
        tall = lax.broadcasted_iota(jnp.int32, (128 - end, 128), 1)
        passed = (tall >= base) & (tall < end)
        for b in range(8):
            here = slice(b * 16, b * 16 + 16)
            x, y, z = split(ub[here])
            left = jnp.concatenate([x, x, y, y, x, z], axis=0)
            x, y, z = split(vb[here])
            right = jnp.concatenate([x, y, x, y, z, x], axis=0)
            change = lax.dot_general(
                left, right, (((0,), (0,)), ((), ())), preferred_element_type=F32
            )
            rows = slice(b * 128 + end, b * 128 + 128)
            st[rows] = jnp.where(passed, 0.0, st[rows]) - change[end:]


def factor_kernel(
    meta, x_ref, d_ref, out_ref, panel_ref, trailing_ref, st, ub, vb, g, f, s, w, ld, lf,
    blank, empty, sems,
):
    blank[...] = jnp.zeros_like(blank)
    empty[...] = jnp.zeros_like(empty)
    fills = [pltpu.make_async_copy(blank, trailing_ref.at[a], sems.at[a]) for a in range(8)]
    fills += [pltpu.make_async_copy(empty, panel_ref.at[p], sems.at[8 + p]) for p in range(2)]
    for fill in fills:
        fill.start()

    def same(i, j):
        return meta[SLOTD + i, j] >= 0

    def held(value, i, j):
        return jnp.where(i // SUPER < j // SUPER, value.astype(BF16).astype(F32), value)

    def block(i, j):
        return d_ref[meta[SLOTD + i, j]]

    st[...] = jnp.zeros_like(st)
    @pl.loop(0, meta[SIZES, 1])
    def _(level):
        @pl.loop(0, PICKS)
        def _(j):
            @pl.when(meta[LEVEL, j] == level)
            def _():
                s[...] = block(j, j)

                @pl.loop(0, j)
                def _(i):
                    @pl.when(same(j, i))
                    def _():
                        w[...] = block(j, i)

                        @pl.loop(0, i)
                        def _(m):
                            @pl.when(same(j, m))
                            def _():
                                w[...] -= dot_nt(
                                    held(f[j * PICKS + m], m, i), held(f[i * PICKS + m], m, i)
                                )

                        done = dot_nt(w[...], g[i])
                        f[j * PICKS + i] = done
                        done = held(done, i, j)
                        s[...] -= dot_nt(done, done)

                st[pl.ds(pl.multiple_of(meta[SPOT, j] * 128, 128), 128)] = s[...]

        batched_inverse(st, ub, vb)

        @pl.loop(0, PICKS)
        def _(j):
            @pl.when(meta[LEVEL, j] == level)
            def _():
                g[j] = st[pl.ds(pl.multiple_of(meta[SPOT, j] * 128, 128), 128)]

    my_row = lax.axis_index("row")
    last = out_ref.shape[0] - 1
    for a in range(8):
        for j in range(PICKS):
            slot = meta[j, a * 16 + my_row]
            ld[j, a * 16 : (a + 1) * 16] = jnp.where(slot >= 0, x_ref[jnp.maximum(slot, 0)], 0.0)

    for j in range(PICKS):
        lf[j] = dot_nt(ld[j], g[j])

    @pl.loop(1, PICKS)
    def _(j):
        @pl.when(meta[LEVEL, j] > 0)
        def _():
            @pl.loop(0, j)
            def _(i):
                @pl.when(same(j, i))
                def _():
                    ld[j] -= dot_nt(held(lf[i], i, j), held(f[j * PICKS + i], i, j))

            lf[j] = dot_nt(ld[j], g[j])

    for a in range(8):
        elim = meta[ELIM, a * 16 + my_row]
        for j in range(PICKS):
            slot = meta[j, a * 16 + my_row]
            alive = (elim < 0) | (elim >= (j // SUPER + 1) * SUPER)
            rows = jnp.where(alive, lf[j, a * 16 : (a + 1) * 16], 0.0)
            out_ref[jnp.where(slot >= 0, slot, last)] = rows.astype(BF16)

    for fill in fills:
        fill.wait()


def factor(meta, x, d):
    slots = x.shape[0]
    vmem = pl.BlockSpec(memory_space=pltpu.VMEM)
    return pl.pallas_call(
        factor_kernel,
        out_shape=(
            jax.ShapeDtypeStruct((slots + 1, 16, 128), BF16),
            jax.ShapeDtypeStruct((2, 8, 8, 16, 512), BF16),
            jax.ShapeDtypeStruct((8, 16, 128, 128), F32),
        ),
        in_specs=[pl.BlockSpec(memory_space=pltpu.SMEM), vmem, vmem],
        out_specs=(vmem, pl.BlockSpec(memory_space=pl.ANY), pl.BlockSpec(memory_space=pl.ANY)),
        scratch_shapes=[
            pltpu.VMEM((1024, 128), F32),
            pltpu.VMEM((128, 128), F32),
            pltpu.VMEM((128, 128), F32),
            pltpu.VMEM((8, 128, 128), F32),
            pltpu.VMEM((64, 128, 128), F32),
            pltpu.VMEM((128, 128), F32),
            pltpu.VMEM((128, 128), F32),
            pltpu.VMEM((8, 128, 128), F32),
            pltpu.VMEM((8, 128, 128), F32),
            pltpu.VMEM((16, 128, 128), F32),
            pltpu.VMEM((8, 8, 16, 512), BF16),
            pltpu.SemaphoreType.DMA((10,)),
        ],
        compiler_params=pltpu.CompilerParams(vmem_limit_bytes=48 << 20),
        name="factor",
    )(meta, x, d.reshape(slots, 128, 128))


def share_kernel(l_ref, row_ref, col_ref, se, qe, sf, qf, sg, qg, sx, qx, sz, qz):
    slots = l_ref.shape[0] - 1
    n = slots // 16
    r, c, y, k = place()
    z, x = r // 4, lax.rem(r, 4)
    other = {"row": r, "col": y * 2 + 1 - k}
    goal = lax.rem(r, 8)
    high = r // 8

    def along(dy):
        return {"row": r, "col": lax.rem(y + dy, 4) * 2 + k}

    def along_x(d):
        return {"row": z * 4 + lax.rem(x + d, 4), "col": c}

    def along_z(d):
        return {"row": lax.rem(z + d, 4) * 4 + x, "col": c}

    def greet(device):
        pl.semaphore_signal(barrier, inc=1, device_id=device, device_id_type=MESH)

    barrier = pltpu.get_barrier_semaphore()
    greet(other)
    for d in (1, 2, 3):
        greet(along(d))
        greet(along_x(d))
        greet(along_z(d))
    for q in range(16):
        source = c + (q // 8) * 8
        far = jnp.logical_not((source == r) & (q % 8 == c))

        @pl.when(far)
        def _():
            greet({"row": source, "col": q % 8})

    pl.semaphore_wait(barrier, 25 + jnp.where(goal == c, 0, 1))

    def send(d):
        m = lax.rem(r + d, 16)
        return pltpu.make_async_remote_copy(
            src_ref=l_ref.at[pl.ds(m * n, n)],
            dst_ref=col_ref.at[high, m // 4, lax.rem(m, 4), :, c],
            send_sem=sg.at[d], recv_sem=qg.at[high * 8 + c],
            device_id={"row": m, "col": goal}, device_id_type=MESH,
        )

    for d in range(1, 16):
        send(d).start()

    @pl.when(goal == c)
    def _():
        col_ref[high, z, x, :, c] = l_ref[pl.ds(r * n, n)]

    @pl.when(goal != c)
    def _():
        send(0).start()

    row_ref[y, k] = l_ref[:slots]
    outs = []
    for d in (2, 1, 3):
        h = pltpu.make_async_remote_copy(
            src_ref=row_ref.at[y, k], dst_ref=row_ref.at[y, k],
            send_sem=se.at[d], recv_sem=qe.at[d], device_id=along(d), device_id_type=MESH,
        )
        h.start()
        outs.append((d, h))

    def move(ref, s, q, device):
        h = pltpu.make_async_remote_copy(
            src_ref=ref, dst_ref=ref, send_sem=s, recv_sem=q, device_id=device, device_id_type=MESH
        )
        h.start()
        return h

    near = []
    for half in range(2):
        for q in range(half * 8, half * 8 + 8):
            far = jnp.logical_not((c + half * 8 == r) & (q % 8 == c))

            @pl.when(far)
            def _():
                pltpu.make_async_remote_copy(
                    src_ref=l_ref.at[pl.ds(0, n)], dst_ref=col_ref.at[half, z, x, :, q % 8],
                    send_sem=sg.at[0], recv_sem=qg.at[q], device_id=other, device_id_type=MESH,
                ).wait_recv()

        for d in (2, 1, 3):
            if half == 0:
                near.append(move(col_ref.at[0, z, x], sx.at[d], qx.at[d], along_x(d)))
            else:
                near.append(move(col_ref.at[1, z, x], sz.at[d], qz.at[d], along_z(d)))

    twins = []
    for d in (0, 1, 3, 2):
        come = lax.rem(y + 4 - d, 4)
        for e, h in outs:
            if e == d:
                h.wait_recv()
        twins.append(move(row_ref.at[come, k], sf.at[d], qf.at[d], other))

    for h in near:
        h.wait_recv()
    last = []
    for d in (2, 1, 3):
        last.append(move(col_ref.at[0, z], sx.at[3 + d], qx.at[3 + d], along_z(d)))
        last.append(move(col_ref.at[1, :, x], sz.at[3 + d], qz.at[3 + d], along_x(d)))
    for h in twins + last:
        h.wait()
    for h in near + [h for _, h in outs]:
        h.wait_send()
    for d in range(1, 16):
        send(d).wait_send()

    @pl.when(goal != c)
    def _():
        send(0).wait_send()


def share(l):
    slots = l.shape[0] - 1
    vmem = pl.BlockSpec(memory_space=pltpu.VMEM)
    dma = pltpu.SemaphoreType.DMA
    return pl.pallas_call(
        share_kernel,
        out_shape=(
            jax.ShapeDtypeStruct((4, 2, slots, 16, 128), BF16),
            jax.ShapeDtypeStruct((2, 4, 4, slots // 16, 8, 16, 128), BF16),
        ),
        in_specs=[vmem],
        out_specs=(vmem, vmem),
        scratch_shapes=[
            dma((4,)), dma((4,)), dma((4,)), dma((4,)), dma((16,)), dma((16,)),
            dma((7,)), dma((7,)), dma((7,)), dma((7,)),
        ],
        compiler_params=pltpu.CompilerParams(
            collective_id=slots + 1, has_side_effects=True, vmem_limit_bytes=48 << 20
        ),
        name="share",
    )(l)


def update_kernel(
    meta, a_ref, row_in, col_in, zero_panel, zero, panel_ref, out_ref, held, done, row_ref, col_ref,
    listed, come, go, out, bring,
):
    my_col = lax.axis_index("col")
    my_row = lax.axis_index("row")
    rows_in = pltpu.make_async_copy(row_in, row_ref, bring.at[0])
    cols_in = pltpu.make_async_copy(col_in, col_ref, bring.at[1])
    rows_in.start()
    cols_in.start()

    def fetch(q):
        code = listed[q]
        return pltpu.make_async_copy(a_ref.at[code // 16, code % 16], held.at[q], come.at[q])

    def store(q):
        code = listed[q]
        return pltpu.make_async_copy(done.at[q], out_ref.at[code // 16, code % 16], go.at[q])

    def row(a, start):
        g = a * 16 + my_row

        def one(n, q):
            listed[q] = a * 16 + meta[LIST + n, g]
            fetch(q).start()
            return q + 1

        return lax.fori_loop(0, meta[HITS, g], one, start)

    total = lax.fori_loop(0, 8, row, 0)

    def each_panel(act):
        @pl.loop(0, 8)
        def _(a):
            g = a * 16 + my_row

            @pl.when(meta[NUMBER, g] > 0)
            def _():
                for j in range(PICKS):
                    slot = meta[j, g]

                    @pl.when(slot >= 0)
                    def _():
                        lanes = pl.ds((j % SUPER) * 128, 128)
                        act(
                            pltpu.make_async_copy(
                                row_ref.at[:, slot],
                                panel_ref.at[j // SUPER, a, :, :, lanes],
                                out.at[slot],
                            )
                        )

    rows_in.wait()
    each_panel(lambda copy: copy.start())
    cols_in.wait()

    def left(slot):
        return row_ref[:, slot].reshape(128, 128)

    def product(x, y):
        return lax.dot_general(x, y, NT, preferred_element_type=F32)

    @pl.loop(0, (total + WAVE - 1) // WAVE)
    def _(t):
        for u in range(WAVE):
            @pl.when(t * WAVE + u < total)
            def _():
                fetch(t * WAVE + u).wait()

        places = [jnp.minimum(t * WAVE + u, total - 1) for u in range(WAVE)]
        results = []
        for q in places:
            g = listed[q] // 16 * 16 + my_row
            b = listed[q] % 16
            h = b * 8 + my_col
            half = b % 2
            number = meta[NUMBER, g]
            x, y = [], []
            for t_row, least in ((ONE, 1), (TWO, 2)):
                x.append(jnp.where(number >= least, left(jnp.maximum(meta[t_row, g], 0)), 0))
                y.append(jnp.where(number >= least, col_ref[half, jnp.maximum(meta[t_row, h], 0)], 0))
            results.append(
                held[q] - product(jnp.concatenate(x, axis=1), jnp.concatenate(y, axis=1))
            )
        for q, result in zip(places, results):
            done[q] = result

        @pl.when(meta[SIZES, 1] > 2)
        def _():
            @pl.loop(t * WAVE, jnp.minimum(t * WAVE + WAVE, total))
            def _(q):
                g = listed[q] // 16 * 16 + my_row
                b = listed[q] % 16

                @pl.when(meta[NUMBER, g] > 2)
                def _():
                    @pl.loop(2, PICKS)
                    def _(j):
                        @pl.when((meta[j, g] >= 0) & (meta[LEVEL, j] >= 2))
                        def _():
                            done[q] -= product(
                                left(meta[j, g]), col_ref[b % 2, meta[j, b * 8 + my_col]]
                            )

        for u in range(WAVE):
            @pl.when(t * WAVE + u < total)
            def _():
                store(t * WAVE + u).start()

    @pl.loop(0, total)
    def _(q):
        store(q).wait()

    each_panel(lambda copy: copy.wait())


def update(meta, blocks, rows, cols, panels, trailing):
    slots = rows.shape[2]
    hbm = pl.BlockSpec(memory_space=pl.ANY)
    return pl.pallas_call(
        update_kernel,
        out_shape=(
            jax.ShapeDtypeStruct(panels.shape, BF16),
            jax.ShapeDtypeStruct(trailing.shape, F32),
        ),
        in_specs=[pl.BlockSpec(memory_space=pltpu.SMEM), hbm, hbm, hbm, hbm, hbm],
        out_specs=(hbm, hbm),
        scratch_shapes=[
            pltpu.VMEM((128, 128, 128), F32),
            pltpu.VMEM((128, 128, 128), F32),
            pltpu.VMEM((8, slots, 16, 128), BF16),
            pltpu.VMEM((2, slots, 128, 128), BF16),
            pltpu.SMEM((128,), jnp.int32),
            pltpu.SemaphoreType.DMA((128,)),
            pltpu.SemaphoreType.DMA((128,)),
            pltpu.SemaphoreType.DMA((slots,)),
            pltpu.SemaphoreType.DMA((2,)),
        ],
        input_output_aliases={4: 0, 5: 1},
        compiler_params=pltpu.CompilerParams(vmem_limit_bytes=48 << 20),
        name="update",
    )(meta, blocks, rows.reshape(8, slots, 16, 128), cols.reshape(2, slots, 128, 128), panels, trailing)


def ranks(marks, before):
    total = jnp.sum(marks, axis=0, keepdims=True)
    run = jnp.dot(jnp.broadcast_to(total, (8, 128)), before, preferred_element_type=F32)[:1]
    rows = []
    for j in range(8):
        rows.append(jnp.where(marks[j : j + 1] > 0, run, -1.0))
        run = run + marks[j : j + 1]
    return jnp.concatenate(rows, axis=0), jnp.max(run, axis=1, keepdims=True)


def tables_kernel(order, pattern_ref, meta_ref, tier_ref):
    lanes = lax.broadcasted_iota(jnp.int32, (8, 128), 1)
    rows = lax.broadcasted_iota(jnp.int32, (8, 128), 0)
    lane = lanes[:1]
    g = lax.broadcasted_iota(jnp.int32, (128, 128), 0)
    h = lax.broadcasted_iota(jnp.int32, (128, 128), 1)
    onehot = jnp.zeros((8, 128), F32)
    target = jnp.zeros((1, 128), jnp.int32)
    for j in range(PICKS):
        onehot = jnp.where((rows == j) & (lanes == order[j]), 1.0, onehot)
        target = jnp.where(lane == j, order[j], target)
    linked = pattern_ref[...].astype(F32)
    pad = lambda x: jnp.concatenate([x, jnp.zeros((120, 128), F32)], axis=0)
    small = lambda a, b: lax.dot_general(a, b, NT, preferred_element_type=F32)
    member = jnp.dot(onehot, linked, preferred_element_type=F32)
    slot, full = ranks(member, (((g & 15) == (h & 15)) & (g < h)).astype(F32))
    among = small(onehot, pad(member))
    lower = jnp.where(lanes <= rows, among, 0.0)
    upper = jnp.where(rows <= lanes, among, 0.0)
    slotd, fulld = ranks(lower, (g < h).astype(F32))
    home = jnp.sum(onehot * (lanes & 15).astype(F32), axis=1, keepdims=True)
    code = home * 64.0 + small(onehot, pad(slot))
    source = jnp.zeros((8, 128), F32)
    for j in range(PICKS):
        source = source + jnp.where(slotd[:, j : j + 1] == lanes.astype(F32), code[:, j : j + 1], 0.0)
    source = jnp.sum(source, axis=0, keepdims=True)
    source = jnp.where(lane.astype(F32) < fulld, source, 1024.0)
    down = jnp.sum(lower, axis=1, keepdims=True) - 1.0
    level = jnp.sum(upper, axis=0, keepdims=True) - 1.0
    spot = jnp.sum(jnp.where((down == level) & (rows < lanes), 1.0, 0.0), axis=0, keepdims=True)
    depth = jnp.max(down, axis=0, keepdims=True) + 1.0
    need = jnp.maximum(full, fulld)
    sizes = jnp.where(lane == 0, need, depth)
    tier = sum((need > slots).astype(F32) for slots in TIERS[:-1])
    tier_ref[0] = jnp.max(tier).astype(jnp.int32)
    elim = jnp.sum(onehot * (rows + 1).astype(F32), axis=0, keepdims=True) - 1.0
    label = jnp.min(jnp.where(linked > 0, g.astype(F32), 999.0), axis=0, keepdims=True)

    def put(row, value):
        meta_ref[row : row + value.shape[0]] = value.astype(jnp.int32)

    put(0, slot)
    put(LABEL, label)
    put(ELIM, elim)
    put(TARGET, target)
    put(LEVEL, level)
    put(SPOT, spot)
    put(SOURCE, source)
    put(SIZES, sizes)
    put(SLOTD, slotd)
    rows16 = lax.broadcasted_iota(jnp.int32, (16, 128), 0)
    lanes16 = lax.broadcasted_iota(jnp.int32, (16, 128), 1)
    mine = (lanes16 == rows16 * 8 + lax.axis_index("col")).astype(F32)
    held = jnp.dot(mine, linked, preferred_element_type=F32)
    run = jnp.zeros((1, 128), F32)
    listed = jnp.zeros((16, 128), F32)
    for b in range(16):
        here = held[b : b + 1]
        listed = jnp.where((here > 0) & (run == rows16.astype(F32)), float(b), listed)
        run = run + here
    put(HITS, run)
    put(LIST, listed)
    put(NUMBER, jnp.sum(member, axis=0, keepdims=True))
    for row, order_in in ((ONE, 0.0), (TWO, 1.0)):
        taken = jnp.where((member > 0) & (down == order_in), slot + 1.0, 0.0)
        put(row, jnp.sum(taken, axis=0, keepdims=True) - 1.0)


def tables(pattern, order):
    vmem = pl.BlockSpec(memory_space=pltpu.VMEM)
    return pl.pallas_call(
        tables_kernel,
        out_shape=(
            jax.ShapeDtypeStruct((48, 128), jnp.int32),
            jax.ShapeDtypeStruct((1,), jnp.int32),
        ),
        in_specs=[pl.BlockSpec(memory_space=pltpu.SMEM), vmem],
        out_specs=(vmem, pl.BlockSpec(memory_space=pltpu.SMEM)),
        name="tables",
    )(order, pattern)


def compact(slots, meta, blocks):
    given = pick(slots, meta, blocks.reshape(8, 16, 8, 16, 128))
    x, d = gather(meta, given)
    l, panels, trailing = factor(meta, x, d)
    rows, cols = share(l)
    panels, trailing = update(meta, blocks, rows, cols, panels, trailing)
    return panels.reshape(2, 8, 128, 512), trailing


def shards(matrix_blocks, pattern, order):
    local = matrix_blocks[:, 0, :, 0]
    meta, tier = tables(pattern, order)
    ways = [functools.partial(compact, slots, meta, local) for slots in TIERS]
    panels, trailing = lax.switch(tier[0], ways)
    return panels[:, :, None], trailing[:, None, :, None]


def solution(mesh):
    in_specs = (P(None, "row", None, "col", None, None), P(), P())
    out_specs = (P(None, None, "row", None, None), P(None, "row", None, "col", None, None))
    return jax.shard_map(shards, mesh=mesh, in_specs=in_specs, out_specs=out_specs, check_vma=False)
```

```python
import functools

import jax
import jax.numpy as jnp
from jax import lax
from jax.experimental import pallas as pl
from jax.experimental.pallas import tpu as pltpu
from jax.sharding import PartitionSpec as P

SUPER = 4
WAVE = 4
PICKS = 8
TIERS = (16, 32, 64)
MESH = pl.DeviceIdType.MESH
HIGH = lax.Precision.HIGHEST
F32 = jnp.float32
BF16 = jnp.bfloat16
NT = (((1,), (1,)), ((), ()))

LABEL = 8
ELIM = 9
TARGET = 10
LEVEL = 11
SPOT = 12
SOURCE = 14
SIZES = 15
NUMBER = 24
ONE = 25
TWO = 26
HITS = 27
LIST = 32
SLOTD = 16


def dot_nt(a, b):
    return lax.dot_general(a, b, NT, precision=HIGH, preferred_element_type=F32)


def pick_kernel(meta, a_ref, out_ref, sems):
    my_row = lax.axis_index("row")
    my_col = lax.axis_index("col")
    out_ref[...] = jnp.zeros_like(out_ref)

    def each(act):
        @pl.loop(0, PICKS)
        def _(j):
            target = meta[TARGET, j]

            @pl.when(target % 8 == my_col)
            def _():
                for a in range(8):
                    slot = meta[j, a * 16 + my_row]

                    @pl.when(slot >= 0)
                    def _():
                        act(
                            pltpu.make_async_copy(
                                a_ref.at[a, target // 8], out_ref.at[:, slot], sems.at[slot]
                            )
                        )

    each(lambda copy: copy.start())
    each(lambda copy: copy.wait())


def pick(slots, meta, blocks):
    return pl.pallas_call(
        pick_kernel,
        out_shape=jax.ShapeDtypeStruct((8, slots, 16, 128), F32),
        in_specs=[pl.BlockSpec(memory_space=pltpu.SMEM), pl.BlockSpec(memory_space=pl.ANY)],
        out_specs=pl.BlockSpec(memory_space=pltpu.VMEM),
        scratch_shapes=[pltpu.SemaphoreType.DMA((slots,))],
        compiler_params=pltpu.CompilerParams(vmem_limit_bytes=24 << 20),
        name="pick",
    )(meta, blocks)


def place():
    r = lax.axis_index("row")
    c = lax.axis_index("col")
    return r, c, c // 2, c % 2


def gather_kernel(
    meta, give_ref, x_ref, d_ref, ra, acc, rb, dsrc, rr, piece,
    sa, qa, sb, qb, sc, qc, sd, qd, se, qe, sf, qf,
):
    slots = x_ref.shape[0]
    r, c, y, k = place()
    other = {"row": r, "col": y * 2 + 1 - k}

    def along(dy):
        return {"row": r, "col": lax.rem(y + dy, 4) * 2 + k}

    def across(dr):
        return {"row": lax.rem(r + dr, 16), "col": c}

    z, x = r // 4, lax.rem(r, 4)

    def along_x(d):
        return {"row": z * 4 + lax.rem(x + d, 4), "col": c}

    def along_z(d):
        return {"row": lax.rem(z + d, 4) * 4 + x, "col": c}

    inside = y // 2 == k

    def to_half(dy):
        return {"row": r, "col": lax.rem(y + dy, 4) * 2 + y // 2}

    barrier = pltpu.get_barrier_semaphore()
    pl.semaphore_signal(barrier, inc=1, device_id=other, device_id_type=MESH)
    for dy in (1, 2, 3):
        pl.semaphore_signal(barrier, inc=1, device_id=along(dy), device_id_type=MESH)
    for dr in range(1, 16):
        pl.semaphore_signal(barrier, inc=1, device_id=across(dr), device_id_type=MESH)
    for q in range(4):
        @pl.when(4 * k + q != c)
        def _():
            pl.semaphore_signal(
                barrier, inc=1, device_id={"row": r, "col": 4 * k + q}, device_id_type=MESH
            )

    pl.semaphore_wait(barrier, 22 + jnp.where(inside, 0, 1))

    halves = []
    for dy in (2, 1, 3, 0):
        there = lax.rem(y + dy, 4)
        h = pltpu.make_async_remote_copy(
            src_ref=give_ref.at[there, 1 - k], dst_ref=ra.at[dy],
            send_sem=sa.at[dy], recv_sem=qa.at[dy], device_id=other, device_id_type=MESH,
        )
        h.start()
        halves.append((dy, there, h))
    quarters = []
    for dy, there, h in halves:
        h.wait_recv()
        if dy:
            acc[dy] = give_ref[there, k] + ra[dy]
            q = pltpu.make_async_remote_copy(
                src_ref=acc.at[dy], dst_ref=rb.at[dy],
                send_sem=sb.at[dy], recv_sem=qb.at[dy], device_id=along(dy), device_id_type=MESH,
            )
            q.start()
            quarters.append((dy, q))
        else:
            total = give_ref[there, k] + ra[dy]
    for dy, q in quarters:
        q.wait_recv()
        total = total + rb[dy]
    x_ref[...] = total

    for d in range(slots):
        code = meta[SOURCE, d]
        mine = (code // 64 == r).astype(F32)
        dsrc[d * 16 : (d + 1) * 16] = x_ref[code % 64] * mine
    parts = []
    for dr in range(1, 16):
        there = lax.rem(r + dr, 16)
        h = pltpu.make_async_remote_copy(
            src_ref=dsrc.at[pl.ds(there * slots, slots)], dst_ref=rr.at[dr],
            send_sem=sc.at[dr], recv_sem=qc.at[dr], device_id=across(dr), device_id_type=MESH,
        )
        h.start()
        parts.append(h)
    total = dsrc[pl.ds(pl.multiple_of(r * slots, 8), slots)]
    for dr, h in zip(range(1, 16), parts):
        h.wait_recv()
        total = total + rr[dr]
    piece[...] = total.reshape(piece.shape)

    outs = []
    for dy in (2, 1, 3):
        h = pltpu.make_async_remote_copy(
            src_ref=piece, dst_ref=d_ref.at[z, x, :, c],
            send_sem=sd.at[dy], recv_sem=qd.at[c], device_id=to_half(dy), device_id_type=MESH,
        )
        h.start()
        outs.append(h)
    near = pltpu.make_async_remote_copy(
        src_ref=piece, dst_ref=d_ref.at[z, x, :, c],
        send_sem=sd.at[0], recv_sem=qd.at[c], device_id=other, device_id_type=MESH,
    )

    @pl.when(inside)
    def _():
        d_ref[z, x, :, c] = piece[...]

    @pl.when(jnp.logical_not(inside))
    def _():
        near.start()

    for q in range(4):
        source = 4 * k + q

        @pl.when(source != c)
        def _():
            pltpu.make_async_remote_copy(
                src_ref=piece, dst_ref=d_ref.at[z, x, :, source],
                send_sem=sd.at[0], recv_sem=qd.at[source], device_id=other, device_id_type=MESH,
            ).wait_recv()

    def move(ref, i, device):
        h = pltpu.make_async_remote_copy(
            src_ref=ref, dst_ref=ref, send_sem=se.at[i], recv_sem=qe.at[i],
            device_id=device, device_id_type=MESH,
        )
        h.start()
        return h

    def twin(ref, i):
        h = pltpu.make_async_remote_copy(
            src_ref=ref, dst_ref=ref, send_sem=sf.at[i], recv_sem=qf.at[i],
            device_id=other, device_id_type=MESH,
        )
        h.start()
        twins.append(h)

    part_x, part_z = pl.ds(4 * k, 2), pl.ds(4 * k + 2, 2)
    near_x, near_z, far_x, far_z, twins = [], [], [], [], []
    for d in (2, 1, 3):
        near_x.append(move(d_ref.at[z, x, :, part_x], d, along_x(d)))
        near_z.append(move(d_ref.at[z, x, :, part_z], 4 + d, along_z(d)))
    for h in near_x:
        h.wait_recv()
    for d in (2, 1, 3):
        far_x.append((d, move(d_ref.at[z, :, :, part_x], 8 + d, along_z(d))))
    for h in near_z:
        h.wait_recv()
    for d in (2, 1, 3):
        far_z.append((d, move(d_ref.at[:, x, :, part_z], 12 + d, along_x(d))))
    twin(d_ref.at[z, :, :, part_x], 0)
    twin(d_ref.at[:, x, :, part_z], 4)
    for i in (1, 2, 0):
        d, h = far_x[i]
        h.wait_recv()
        twin(d_ref.at[lax.rem(z + 4 - d, 4), :, :, part_x], d)
        d, h = far_z[i]
        h.wait_recv()
        twin(d_ref.at[:, lax.rem(x + 4 - d, 4), :, part_z], 4 + d)
    wholes = near_x + near_z + [h for _, h in far_x + far_z]
    for t in twins:
        t.wait()
    for _, _, h in halves:
        h.wait_send()
    for _, q in quarters:
        q.wait_send()
    for h in parts + wholes + outs:
        h.wait_send()

    @pl.when(jnp.logical_not(inside))
    def _():
        near.wait_send()


def gather(meta, given):
    slots = given.shape[1]
    vmem = pl.BlockSpec(memory_space=pltpu.VMEM)
    dma = pltpu.SemaphoreType.DMA
    return pl.pallas_call(
        gather_kernel,
        out_shape=(
            jax.ShapeDtypeStruct((slots, 16, 128), F32),
            jax.ShapeDtypeStruct((4, 4, slots // 16, 8, 16, 128), F32),
        ),
        in_specs=[pl.BlockSpec(memory_space=pltpu.SMEM), vmem],
        out_specs=(vmem, vmem),
        scratch_shapes=[
            pltpu.VMEM((4, slots, 16, 128), F32),
            pltpu.VMEM((4, slots, 16, 128), F32),
            pltpu.VMEM((4, slots, 16, 128), F32),
            pltpu.VMEM((slots * 16, 128), F32),
            pltpu.VMEM((16, slots, 128), F32),
            pltpu.VMEM((slots // 16, 16, 128), F32),
            dma((4,)), dma((4,)), dma((4,)), dma((4,)),
            dma((16,)), dma((16,)), dma((4,)), dma((8,)),
            dma((16,)), dma((16,)), dma((8,)), dma((8,)),
        ],
        compiler_params=pltpu.CompilerParams(
            collective_id=slots, has_side_effects=True, vmem_limit_bytes=48 << 20
        ),
        name="gather",
    )(meta, given.reshape(4, 2, slots, 16, 128))


def lane(x, i):
    if isinstance(i, int):
        return jnp.broadcast_to(x[:, i : i + 1], x.shape)
    return jnp.take_along_axis(x, jnp.full(x.shape, i, jnp.int32), axis=1)


def pivots(us, vs, first):
    e = {}
    for i in range(8):
        for k in range(i + 1):
            e[i, k] = lane(us[i], first + k)
    f = {}
    for k in range(8):
        f[k, k] = lax.rsqrt(e[k, k])
        for i in range(k + 1, 8):
            f[i, k] = e[i, k] * f[k, k]
        for i in range(k + 1, 8):
            for m in range(k + 1, i + 1):
                e[i, m] = e[i, m] - f[i, k] * f[m, k]
    outs, outv = [], []
    for k in range(8):
        u, v = us[k], vs[k]
        for m in range(k):
            u = u - f[k, m] * outs[m]
            v = v - f[k, m] * outv[m]
        outs.append(u * f[k, k])
        outv.append(v * f[k, k])
    return outs, outv


def split(x):
    high = x.astype(BF16)
    x = x - high.astype(F32)
    middle = x.astype(BF16)
    return high, middle, (x - middle.astype(F32)).astype(BF16)


def batched_inverse(st, ub, vb):
    lanes = lax.broadcasted_iota(jnp.int32, (8, 128), 1)
    for c in range(8):
        base, end = c * 16, c * 16 + 16
        us = [st[pl.ds(base + k, 8, stride=128)] for k in range(16)]
        vs = [
            jnp.where(lanes < base, us[k], (lanes == base + k).astype(F32)) for k in range(16)
        ]
        us[:8], vs[:8] = pivots(us[:8], vs[:8], base)
        for m in range(8, 16):
            for k in range(8):
                w = lane(us[k], base + m)
                us[m] = us[m] - w * us[k]
                vs[m] = vs[m] - w * vs[k]
        us[8:], vs[8:] = pivots(us[8:], vs[8:], base + 8)
        for k in range(16):
            st[pl.ds(base + k, 8, stride=128)] = vs[k]
            ub[pl.ds(k, 8, stride=16)] = jnp.where(lanes < end, 0.0, us[k])
            vb[pl.ds(k, 8, stride=16)] = jnp.where(lanes < end, vs[k], us[k])
        if c == 7:
            continue
        tall = lax.broadcasted_iota(jnp.int32, (128 - end, 128), 1)
        passed = (tall >= base) & (tall < end)
        for b in range(8):
            here = slice(b * 16, b * 16 + 16)
            x, y, z = split(ub[here])
            left = jnp.concatenate([x, x, y, y, x, z], axis=0)
            x, y, z = split(vb[here])
            right = jnp.concatenate([x, y, x, y, z, x], axis=0)
            change = lax.dot_general(
                left, right, (((0,), (0,)), ((), ())), preferred_element_type=F32
            )
            rows = slice(b * 128 + end, b * 128 + 128)
            st[rows] = jnp.where(passed, 0.0, st[rows]) - change[end:]


def factor_kernel(
    meta, x_ref, d_ref, out_ref, panel_ref, trailing_ref, st, ub, vb, g, f, s, w, ld, lf,
    blank, empty, sems,
):
    blank[...] = jnp.zeros_like(blank)
    empty[...] = jnp.zeros_like(empty)
    fills = [pltpu.make_async_copy(blank, trailing_ref.at[a], sems.at[a]) for a in range(8)]
    fills += [pltpu.make_async_copy(empty, panel_ref.at[p], sems.at[8 + p]) for p in range(2)]
    for fill in fills:
        fill.start()

    def same(i, j):
        return meta[SLOTD + i, j] >= 0

    def held(value, i, j):
        return jnp.where(i // SUPER < j // SUPER, value.astype(BF16).astype(F32), value)

    def block(i, j):
        return d_ref[meta[SLOTD + i, j]]

    st[...] = jnp.zeros_like(st)
    @pl.loop(0, meta[SIZES, 1])
    def _(level):
        @pl.loop(0, PICKS)
        def _(j):
            @pl.when(meta[LEVEL, j] == level)
            def _():
                s[...] = block(j, j)

                @pl.loop(0, j)
                def _(i):
                    @pl.when(same(j, i))
                    def _():
                        w[...] = block(j, i)

                        @pl.loop(0, i)
                        def _(m):
                            @pl.when(same(j, m))
                            def _():
                                w[...] -= dot_nt(
                                    held(f[j * PICKS + m], m, i), held(f[i * PICKS + m], m, i)
                                )

                        done = dot_nt(w[...], g[i])
                        f[j * PICKS + i] = done
                        done = held(done, i, j)
                        s[...] -= dot_nt(done, done)

                st[pl.ds(pl.multiple_of(meta[SPOT, j] * 128, 128), 128)] = s[...]

        batched_inverse(st, ub, vb)

        @pl.loop(0, PICKS)
        def _(j):
            @pl.when(meta[LEVEL, j] == level)
            def _():
                g[j] = st[pl.ds(pl.multiple_of(meta[SPOT, j] * 128, 128), 128)]

    my_row = lax.axis_index("row")
    last = out_ref.shape[0] - 1
    for a in range(8):
        for j in range(PICKS):
            slot = meta[j, a * 16 + my_row]
            ld[j, a * 16 : (a + 1) * 16] = jnp.where(slot >= 0, x_ref[jnp.maximum(slot, 0)], 0.0)

    for j in range(PICKS):
        lf[j] = dot_nt(ld[j], g[j])

    @pl.loop(1, PICKS)
    def _(j):
        @pl.when(meta[LEVEL, j] > 0)
        def _():
            @pl.loop(0, j)
            def _(i):
                @pl.when(same(j, i))
                def _():
                    ld[j] -= dot_nt(held(lf[i], i, j), held(f[j * PICKS + i], i, j))

            lf[j] = dot_nt(ld[j], g[j])

    for a in range(8):
        elim = meta[ELIM, a * 16 + my_row]
        for j in range(PICKS):
            slot = meta[j, a * 16 + my_row]
            alive = (elim < 0) | (elim >= (j // SUPER + 1) * SUPER)
            rows = jnp.where(alive, lf[j, a * 16 : (a + 1) * 16], 0.0)
            out_ref[jnp.where(slot >= 0, slot, last)] = rows.astype(BF16)

    for fill in fills:
        fill.wait()


def factor(meta, x, d):
    slots = x.shape[0]
    vmem = pl.BlockSpec(memory_space=pltpu.VMEM)
    return pl.pallas_call(
        factor_kernel,
        out_shape=(
            jax.ShapeDtypeStruct((slots + 1, 16, 128), BF16),
            jax.ShapeDtypeStruct((2, 8, 8, 16, 512), BF16),
            jax.ShapeDtypeStruct((8, 16, 128, 128), F32),
        ),
        in_specs=[pl.BlockSpec(memory_space=pltpu.SMEM), vmem, vmem],
        out_specs=(vmem, pl.BlockSpec(memory_space=pl.ANY), pl.BlockSpec(memory_space=pl.ANY)),
        scratch_shapes=[
            pltpu.VMEM((1024, 128), F32),
            pltpu.VMEM((128, 128), F32),
            pltpu.VMEM((128, 128), F32),
            pltpu.VMEM((8, 128, 128), F32),
            pltpu.VMEM((64, 128, 128), F32),
            pltpu.VMEM((128, 128), F32),
            pltpu.VMEM((128, 128), F32),
            pltpu.VMEM((8, 128, 128), F32),
            pltpu.VMEM((8, 128, 128), F32),
            pltpu.VMEM((16, 128, 128), F32),
            pltpu.VMEM((8, 8, 16, 512), BF16),
            pltpu.SemaphoreType.DMA((10,)),
        ],
        compiler_params=pltpu.CompilerParams(vmem_limit_bytes=48 << 20),
        name="factor",
    )(meta, x, d.reshape(slots, 128, 128))


def share_kernel(l_ref, row_ref, col_ref, se, qe, sf, qf, sg, qg, sx, qx, sz, qz):
    slots = l_ref.shape[0] - 1
    n = slots // 16
    r, c, y, k = place()
    z, x = r // 4, lax.rem(r, 4)
    other = {"row": r, "col": y * 2 + 1 - k}
    goal = lax.rem(r, 8)
    high = r // 8

    def along(dy):
        return {"row": r, "col": lax.rem(y + dy, 4) * 2 + k}

    def along_x(d):
        return {"row": z * 4 + lax.rem(x + d, 4), "col": c}

    def along_z(d):
        return {"row": lax.rem(z + d, 4) * 4 + x, "col": c}

    def greet(device):
        pl.semaphore_signal(barrier, inc=1, device_id=device, device_id_type=MESH)

    barrier = pltpu.get_barrier_semaphore()
    greet(other)
    for d in (1, 2, 3):
        greet(along(d))
        greet(along_x(d))
        greet(along_z(d))
    for q in range(16):
        source = c + (q // 8) * 8
        far = jnp.logical_not((source == r) & (q % 8 == c))

        @pl.when(far)
        def _():
            greet({"row": source, "col": q % 8})

    pl.semaphore_wait(barrier, 25 + jnp.where(goal == c, 0, 1))

    def send(d):
        m = lax.rem(r + d, 16)
        return pltpu.make_async_remote_copy(
            src_ref=l_ref.at[pl.ds(m * n, n)],
            dst_ref=col_ref.at[high, m // 4, lax.rem(m, 4), :, c],
            send_sem=sg.at[d], recv_sem=qg.at[high * 8 + c],
            device_id={"row": m, "col": goal}, device_id_type=MESH,
        )

    for d in range(1, 16):
        send(d).start()

    @pl.when(goal == c)
    def _():
        col_ref[high, z, x, :, c] = l_ref[pl.ds(r * n, n)]

    @pl.when(goal != c)
    def _():
        send(0).start()

    row_ref[y, k] = l_ref[:slots]
    outs = []
    for d in (2, 1, 3):
        h = pltpu.make_async_remote_copy(
            src_ref=row_ref.at[y, k], dst_ref=row_ref.at[y, k],
            send_sem=se.at[d], recv_sem=qe.at[d], device_id=along(d), device_id_type=MESH,
        )
        h.start()
        outs.append((d, h))

    def move(ref, s, q, device):
        h = pltpu.make_async_remote_copy(
            src_ref=ref, dst_ref=ref, send_sem=s, recv_sem=q, device_id=device, device_id_type=MESH
        )
        h.start()
        return h

    near = []
    for half in range(2):
        for q in range(half * 8, half * 8 + 8):
            far = jnp.logical_not((c + half * 8 == r) & (q % 8 == c))

            @pl.when(far)
            def _():
                pltpu.make_async_remote_copy(
                    src_ref=l_ref.at[pl.ds(0, n)], dst_ref=col_ref.at[half, z, x, :, q % 8],
                    send_sem=sg.at[0], recv_sem=qg.at[q], device_id=other, device_id_type=MESH,
                ).wait_recv()

        for d in (2, 1, 3):
            if half == 0:
                near.append(move(col_ref.at[0, z, x], sx.at[d], qx.at[d], along_x(d)))
            else:
                near.append(move(col_ref.at[1, z, x], sz.at[d], qz.at[d], along_z(d)))

    last = []
    for e, i in ((0, None), (1, 1), (3, 2), (2, 0)):
        if e:
            near[i].wait_recv()
        part = col_ref.at[0, z, lax.rem(x + 4 - e, 4)]
        for d in (2, 1, 3):
            last.append(move(part, sx.at[d * 4 + e], qx.at[d * 4 + e], along_z(d)))
        if e:
            near[3 + i].wait_recv()
        part = col_ref.at[1, lax.rem(z + 4 - e, 4), x]
        for d in (2, 1, 3):
            last.append(move(part, sz.at[d * 4 + e], qz.at[d * 4 + e], along_x(d)))

    twins = []
    for d in (0, 1, 3, 2):
        come = lax.rem(y + 4 - d, 4)
        for e, h in outs:
            if e == d:
                h.wait_recv()
        twins.append(move(row_ref.at[come, k], sf.at[d], qf.at[d], other))

    for h in twins + last:
        h.wait()
    for h in near + [h for _, h in outs]:
        h.wait_send()
    for d in range(1, 16):
        send(d).wait_send()

    @pl.when(goal != c)
    def _():
        send(0).wait_send()


def share(l):
    slots = l.shape[0] - 1
    vmem = pl.BlockSpec(memory_space=pltpu.VMEM)
    dma = pltpu.SemaphoreType.DMA
    return pl.pallas_call(
        share_kernel,
        out_shape=(
            jax.ShapeDtypeStruct((4, 2, slots, 16, 128), BF16),
            jax.ShapeDtypeStruct((2, 4, 4, slots // 16, 8, 16, 128), BF16),
        ),
        in_specs=[vmem],
        out_specs=(vmem, vmem),
        scratch_shapes=[
            dma((4,)), dma((4,)), dma((4,)), dma((4,)), dma((16,)), dma((16,)),
            dma((16,)), dma((16,)), dma((16,)), dma((16,)),
        ],
        compiler_params=pltpu.CompilerParams(
            collective_id=slots + 1, has_side_effects=True, vmem_limit_bytes=48 << 20
        ),
        name="share",
    )(l)


def update_kernel(
    meta, a_ref, row_in, col_in, zero_panel, zero, panel_ref, out_ref, held, done, row_ref, col_ref,
    listed, come, go, out, bring,
):
    my_col = lax.axis_index("col")
    my_row = lax.axis_index("row")
    rows_in = pltpu.make_async_copy(row_in, row_ref, bring.at[0])
    cols_in = pltpu.make_async_copy(col_in, col_ref, bring.at[1])
    rows_in.start()
    cols_in.start()

    def fetch(q):
        code = listed[q]
        return pltpu.make_async_copy(a_ref.at[code // 16, code % 16], held.at[q], come.at[q])

    def store(q):
        code = listed[q]
        return pltpu.make_async_copy(done.at[q], out_ref.at[code // 16, code % 16], go.at[q])

    def row(a, start):
        g = a * 16 + my_row

        def one(n, q):
            listed[q] = a * 16 + meta[LIST + n, g]
            fetch(q).start()
            return q + 1

        return lax.fori_loop(0, meta[HITS, g], one, start)

    total = lax.fori_loop(0, 8, row, 0)

    def each_panel(act):
        @pl.loop(0, 8)
        def _(a):
            g = a * 16 + my_row

            @pl.when(meta[NUMBER, g] > 0)
            def _():
                for j in range(PICKS):
                    slot = meta[j, g]

                    @pl.when(slot >= 0)
                    def _():
                        lanes = pl.ds((j % SUPER) * 128, 128)
                        act(
                            pltpu.make_async_copy(
                                row_ref.at[:, slot],
                                panel_ref.at[j // SUPER, a, :, :, lanes],
                                out.at[slot],
                            )
                        )

    rows_in.wait()
    each_panel(lambda copy: copy.start())
    cols_in.wait()

    def left(slot):
        return row_ref[:, slot].reshape(128, 128)

    def product(x, y):
        return lax.dot_general(x, y, NT, preferred_element_type=F32)

    @pl.loop(0, (total + WAVE - 1) // WAVE)
    def _(t):
        for u in range(WAVE):
            @pl.when(t * WAVE + u < total)
            def _():
                fetch(t * WAVE + u).wait()

        places = [jnp.minimum(t * WAVE + u, total - 1) for u in range(WAVE)]
        results = []
        for q in places:
            g = listed[q] // 16 * 16 + my_row
            b = listed[q] % 16
            h = b * 8 + my_col
            half = b % 2
            number = meta[NUMBER, g]
            x, y = [], []
            for t_row, least in ((ONE, 1), (TWO, 2)):
                x.append(jnp.where(number >= least, left(jnp.maximum(meta[t_row, g], 0)), 0))
                y.append(jnp.where(number >= least, col_ref[half, jnp.maximum(meta[t_row, h], 0)], 0))
            results.append(
                held[q] - product(jnp.concatenate(x, axis=1), jnp.concatenate(y, axis=1))
            )
        for q, result in zip(places, results):
            done[q] = result

        @pl.when(meta[SIZES, 1] > 2)
        def _():
            @pl.loop(t * WAVE, jnp.minimum(t * WAVE + WAVE, total))
            def _(q):
                g = listed[q] // 16 * 16 + my_row
                b = listed[q] % 16

                @pl.when(meta[NUMBER, g] > 2)
                def _():
                    @pl.loop(2, PICKS)
                    def _(j):
                        @pl.when((meta[j, g] >= 0) & (meta[LEVEL, j] >= 2))
                        def _():
                            done[q] -= product(
                                left(meta[j, g]), col_ref[b % 2, meta[j, b * 8 + my_col]]
                            )

        for u in range(WAVE):
            @pl.when(t * WAVE + u < total)
            def _():
                store(t * WAVE + u).start()

    @pl.loop(0, total)
    def _(q):
        store(q).wait()

    each_panel(lambda copy: copy.wait())


def update(meta, blocks, rows, cols, panels, trailing):
    slots = rows.shape[2]
    hbm = pl.BlockSpec(memory_space=pl.ANY)
    return pl.pallas_call(
        update_kernel,
        out_shape=(
            jax.ShapeDtypeStruct(panels.shape, BF16),
            jax.ShapeDtypeStruct(trailing.shape, F32),
        ),
        in_specs=[pl.BlockSpec(memory_space=pltpu.SMEM), hbm, hbm, hbm, hbm, hbm],
        out_specs=(hbm, hbm),
        scratch_shapes=[
            pltpu.VMEM((128, 128, 128), F32),
            pltpu.VMEM((128, 128, 128), F32),
            pltpu.VMEM((8, slots, 16, 128), BF16),
            pltpu.VMEM((2, slots, 128, 128), BF16),
            pltpu.SMEM((128,), jnp.int32),
            pltpu.SemaphoreType.DMA((128,)),
            pltpu.SemaphoreType.DMA((128,)),
            pltpu.SemaphoreType.DMA((slots,)),
            pltpu.SemaphoreType.DMA((2,)),
        ],
        input_output_aliases={4: 0, 5: 1},
        compiler_params=pltpu.CompilerParams(vmem_limit_bytes=48 << 20),
        name="update",
    )(meta, blocks, rows.reshape(8, slots, 16, 128), cols.reshape(2, slots, 128, 128), panels, trailing)


def ranks(marks, before):
    total = jnp.sum(marks, axis=0, keepdims=True)
    run = jnp.dot(jnp.broadcast_to(total, (8, 128)), before, preferred_element_type=F32)[:1]
    rows = []
    for j in range(8):
        rows.append(jnp.where(marks[j : j + 1] > 0, run, -1.0))
        run = run + marks[j : j + 1]
    return jnp.concatenate(rows, axis=0), jnp.max(run, axis=1, keepdims=True)


def tables_kernel(order, pattern_ref, meta_ref, tier_ref):
    lanes = lax.broadcasted_iota(jnp.int32, (8, 128), 1)
    rows = lax.broadcasted_iota(jnp.int32, (8, 128), 0)
    lane = lanes[:1]
    g = lax.broadcasted_iota(jnp.int32, (128, 128), 0)
    h = lax.broadcasted_iota(jnp.int32, (128, 128), 1)
    onehot = jnp.zeros((8, 128), F32)
    target = jnp.zeros((1, 128), jnp.int32)
    for j in range(PICKS):
        onehot = jnp.where((rows == j) & (lanes == order[j]), 1.0, onehot)
        target = jnp.where(lane == j, order[j], target)
    linked = pattern_ref[...].astype(F32)
    pad = lambda x: jnp.concatenate([x, jnp.zeros((120, 128), F32)], axis=0)
    small = lambda a, b: lax.dot_general(a, b, NT, preferred_element_type=F32)
    member = jnp.dot(onehot, linked, preferred_element_type=F32)
    slot, full = ranks(member, (((g & 15) == (h & 15)) & (g < h)).astype(F32))
    among = small(onehot, pad(member))
    lower = jnp.where(lanes <= rows, among, 0.0)
    upper = jnp.where(rows <= lanes, among, 0.0)
    slotd, fulld = ranks(lower, (g < h).astype(F32))
    home = jnp.sum(onehot * (lanes & 15).astype(F32), axis=1, keepdims=True)
    code = home * 64.0 + small(onehot, pad(slot))
    source = jnp.zeros((8, 128), F32)
    for j in range(PICKS):
        source = source + jnp.where(slotd[:, j : j + 1] == lanes.astype(F32), code[:, j : j + 1], 0.0)
    source = jnp.sum(source, axis=0, keepdims=True)
    source = jnp.where(lane.astype(F32) < fulld, source, 1024.0)
    down = jnp.sum(lower, axis=1, keepdims=True) - 1.0
    level = jnp.sum(upper, axis=0, keepdims=True) - 1.0
    spot = jnp.sum(jnp.where((down == level) & (rows < lanes), 1.0, 0.0), axis=0, keepdims=True)
    depth = jnp.max(down, axis=0, keepdims=True) + 1.0
    need = jnp.maximum(full, fulld)
    sizes = jnp.where(lane == 0, need, depth)
    tier = sum((need > slots).astype(F32) for slots in TIERS[:-1])
    tier_ref[0] = jnp.max(tier).astype(jnp.int32)
    elim = jnp.sum(onehot * (rows + 1).astype(F32), axis=0, keepdims=True) - 1.0
    label = jnp.min(jnp.where(linked > 0, g.astype(F32), 999.0), axis=0, keepdims=True)

    def put(row, value):
        meta_ref[row : row + value.shape[0]] = value.astype(jnp.int32)

    put(0, slot)
    put(LABEL, label)
    put(ELIM, elim)
    put(TARGET, target)
    put(LEVEL, level)
    put(SPOT, spot)
    put(SOURCE, source)
    put(SIZES, sizes)
    put(SLOTD, slotd)
    rows16 = lax.broadcasted_iota(jnp.int32, (16, 128), 0)
    lanes16 = lax.broadcasted_iota(jnp.int32, (16, 128), 1)
    mine = (lanes16 == rows16 * 8 + lax.axis_index("col")).astype(F32)
    held = jnp.dot(mine, linked, preferred_element_type=F32)
    run = jnp.zeros((1, 128), F32)
    listed = jnp.zeros((16, 128), F32)
    for b in range(16):
        here = held[b : b + 1]
        listed = jnp.where((here > 0) & (run == rows16.astype(F32)), float(b), listed)
        run = run + here
    put(HITS, run)
    put(LIST, listed)
    put(NUMBER, jnp.sum(member, axis=0, keepdims=True))
    for row, order_in in ((ONE, 0.0), (TWO, 1.0)):
        taken = jnp.where((member > 0) & (down == order_in), slot + 1.0, 0.0)
        put(row, jnp.sum(taken, axis=0, keepdims=True) - 1.0)


def tables(pattern, order):
    vmem = pl.BlockSpec(memory_space=pltpu.VMEM)
    return pl.pallas_call(
        tables_kernel,
        out_shape=(
            jax.ShapeDtypeStruct((48, 128), jnp.int32),
            jax.ShapeDtypeStruct((1,), jnp.int32),
        ),
        in_specs=[pl.BlockSpec(memory_space=pltpu.SMEM), vmem],
        out_specs=(vmem, pl.BlockSpec(memory_space=pltpu.SMEM)),
        name="tables",
    )(order, pattern)


def compact(slots, meta, blocks):
    given = pick(slots, meta, blocks.reshape(8, 16, 8, 16, 128))
    x, d = gather(meta, given)
    l, panels, trailing = factor(meta, x, d)
    rows, cols = share(l)
    panels, trailing = update(meta, blocks, rows, cols, panels, trailing)
    return panels.reshape(2, 8, 128, 512), trailing


def shards(matrix_blocks, pattern, order):
    local = matrix_blocks[:, 0, :, 0]
    meta, tier = tables(pattern, order)
    ways = [functools.partial(compact, slots, meta, local) for slots in TIERS]
    panels, trailing = lax.switch(tier[0], ways)
    return panels[:, :, None], trailing[:, None, :, None]


def solution(mesh):
    in_specs = (P(None, "row", None, "col", None, None), P(), P())
    out_specs = (P(None, None, "row", None, None), P(None, "row", None, "col", None, None))
    return jax.shard_map(shards, mesh=mesh, in_specs=in_specs, out_specs=out_specs, check_vma=False)
```
